256 devices in a mesh: dp: 16 (over x, z_hi, core), fsdp: 16 (over y, z_lo).
Axes of the slice: x: 4, y: 4, z: 8 (z_hi: 2, z_lo: 4; z = z_hi * 4 + z_lo), core: 2. Of those that a mesh axis runs over, the one named last changes fastest.
Arguments:
- latent: bfloat16 [65536, 512], P(('dp', 'fsdp')), may hold values from -6 to 6
- cotangent: bfloat16 [65536, 16384], P(('dp', 'fsdp')), may hold values from -5 to 5
- quant: bfloat16 [512, 16384], P(None, 'fsdp'), may hold values from -6 to 6
- scales: float32 [4, 128], P(None, 'fsdp'), may hold values from 0.015 to 0.09
- adapter_down: bfloat16 [512, 64], replicated, may hold values from -0.25 to 0.25
- adapter_up: bfloat16 [64, 16384], P(None, 'fsdp'), may hold values from -0.75 to 0.75
Outputs:
- latent_gradient: bfloat16 [65536, 512], P(('dp', 'fsdp'))
- grad_a: float32 [512, 64], replicated
- grad_b: float32 [64, 16384], P(None, 'fsdp')
The draws below stay inside these ranges and needn't reach their ends.
All inputs are finite; a program needn't handle non-finite values.
Results may differ from the reference program's by a relative error of at most 0.0049.
Values may be sent and summed in bfloat16 or wider, within the bound.
A program may use at most 128 MiB of HBM per device.

```python
import math
import jax
import jax.numpy as jnp

LATENT_WIDTH = 512
ADAPTER_RANK = 64
BLOCK = 128
OUTPUT_COLUMNS = 16384
TOKENS = 65536


def strengthened(result, own_key, source, target, shards_of, factor):
    owner, partner = [(jnp.arange(result.shape[axis_at]) // (result.shape[axis_at] // shards_of)).reshape([-1 if axis == axis_at else 1 for axis in range(result.ndim)]) for axis_at in (source, target)]
    chosen = jax.random.permutation(own_key, shards_of)[partner]
    strong = (owner == chosen) | (owner == (partner + shards_of // 2) % shards_of)
    return jnp.where(strong, factor * result, result)


def steps_of(stream_key, shape, shards, low, top_value):
    def one(position, shards_of):
        heights = jax.random.uniform(jax.random.fold_in(jax.random.fold_in(stream_key, 6), position), (shards_of,), jnp.float32, low / len(shards), top_value / len(shards))
        return jnp.repeat(jnp.exp(heights), shape[position] // shards_of).reshape((-1,) + (1,) * (len(shape) - position - 1))

    gain = one(*shards[0])
    for cut in shards[1:]:
        gain = gain * one(*cut)
    return gain


def centred(stream_key, dims, deviation, limit, pieces=(), kind=jnp.bfloat16):
    loudness = steps_of(stream_key, dims, pieces, -0.22, 0.18) if pieces else 1.0
    drawn = jax.random.normal(stream_key, dims, jnp.float32) * deviation * loudness
    return jnp.minimum(jnp.maximum(drawn, -limit), limit).astype(kind)


def bell_draw_with(rng, extent, spread, most, cuts, heavy, dtype=jnp.bfloat16):
    entries = spread * jax.random.normal(rng, extent, jnp.float32)
    if cuts:
        entries = entries * steps_of(rng, extent, cuts, -0.22, 0.18)
    return jnp.clip(strengthened(entries, jax.random.fold_in(rng, 3), *heavy), -most, most).astype(dtype)


def setup_inputs(seed: int = 0) -> dict:
    streams_of = jax.random.split(jax.random.key(seed), 7)
    return {
        "latent": centred(streams_of[0], (TOKENS, LATENT_WIDTH), 1.0, 6.0, ((0, 256),)),
        "cotangent": bell_draw_with(streams_of[1], (TOKENS, OUTPUT_COLUMNS), 0.2, 5.0, ((0, 256),), (0, 1, 256, 6.0)),
        "quant": centred(streams_of[2], (LATENT_WIDTH, OUTPUT_COLUMNS), 1.0, 6.0, ((1, 16),)),
        "scales": jnp.clip(jnp.exp(math.log(0.09) - 1.7917595 * jax.random.uniform(streams_of[3], (LATENT_WIDTH // BLOCK, OUTPUT_COLUMNS // BLOCK), jnp.float32) ** steps_of(streams_of[3], (LATENT_WIDTH // BLOCK, OUTPUT_COLUMNS // BLOCK), ((1, 16),), -0.2, 0.2)), 0.015, 0.09),
        "adapter_down": centred(streams_of[4], (LATENT_WIDTH, ADAPTER_RANK), LATENT_WIDTH ** -0.5, 0.25),
        "adapter_up": centred(streams_of[5], (ADAPTER_RANK, OUTPUT_COLUMNS), ADAPTER_RANK ** -0.5, 0.75, ((1, 16),)),
    }


def expand(scales):
    return jnp.repeat(jnp.repeat(scales, BLOCK, axis=0), BLOCK, axis=1)

def reference(latent, cotangent, quant, scales, adapter_down, adapter_up):
    weight = (quant.astype(jnp.float32) * expand(scales)).astype(jnp.bfloat16)
    lowrank_term = jnp.dot(latent, adapter_down, preferred_element_type=jnp.float32).astype(jnp.bfloat16)
    adapter_pass = jnp.dot(cotangent, adapter_up.T, preferred_element_type=jnp.float32).astype(jnp.bfloat16)
    frozen_term = jnp.dot(cotangent, weight.T, preferred_element_type=jnp.float32)
    latent_gradient = (frozen_term + jnp.dot(adapter_pass, adapter_down.T, preferred_element_type=jnp.float32)).astype(jnp.bfloat16)
    factor = 1.0 / jnp.sqrt(jnp.float32(TOKENS))
    grad_a = jnp.dot(latent.T, adapter_pass, preferred_element_type=jnp.float32) * factor
    grad_b = jnp.dot(lowrank_term.T, cotangent, preferred_element_type=jnp.float32) * factor
    return (latent_gradient, grad_a, grad_b)
```

```python
import jax
import jax.numpy as jnp
from jax import lax
from jax.experimental import pallas as pl
from jax.experimental.pallas import tpu as pltpu
from jax.sharding import PartitionSpec as P

MESH = pl.DeviceIdType.MESH
BLOCK = 128
NX, NY, NZ, NC = 4, 4, 8, 2
NS = 4
TOK, COLS, LAT, RANK = 256, 16384, 512, 64
SHARD = COLS // (NY * NS)
QUART = SHARD // 4
HALF = RANK // 2
EXCL = 128
FETCH = LAT - EXCL
TOTAL = 65536
GROUPS = 4

SENDS = 224
RECVS = 224

ORDER = [
    (-1, 0), (1, 0), (0, -1), (0, 1), (2, 0),
    (-1, -1), (-1, 1), (1, -1), (1, 1),
    (0, 2), (2, -1), (2, 1), (-1, 2), (1, 2), (2, 2),
]


def dot_cols(left, right):
    return lax.dot_general(
        left, right, (((1,), (1,)), ((), ())), preferred_element_type=jnp.float32
    )


def kernel(
    scales, latent, cot_hbm, quant, down, up,
    out_lat, out_a, out_b,
    cot, wbuf, ubuf, low_t, acc, thr, own, sib_out, sib_in, x_out, x_in, y_own, y_in,
    z_own, z_in, gath, a_own, a_in, ay_own, ay_in, az_in, ay_all, a_all,
    load_sem, send_sem, recv_sem,
):
    d, f = lax.axis_index("dp"), lax.axis_index("fsdp")
    x, c = lax.div(d, 4), lax.rem(d, 2)
    y, zl = lax.div(f, 4), lax.rem(f, 4)
    z = lax.rem(lax.div(d, 2), 2) * 4 + zl
    par = lax.rem(x, 2)
    me8 = x * 2 + c

    def dev(xx, yy, zz, cc):
        return (xx * 4 + lax.div(zz, 4) * 2 + cc, yy * 4 + lax.rem(zz, 4))

    def at_x(k):
        return dev(lax.rem(x + k + NX, NX), y, z, c)

    def at_y(k):
        return dev(x, lax.rem(y + k + NY, NY), z, c)

    def at_z(k):
        return dev(x, y, lax.rem(z + k + NZ, NZ), c)

    def at_8(k):
        p = lax.rem(me8 + k, 8)
        return dev(lax.div(p, 2), y, z, lax.rem(p, 2))

    sibling = dev(x, y, z, 1 - c)

    sent = []
    events = {}

    def event(name):
        return recv_sem.at[events.setdefault(name, len(events))]

    def send(name, src, dst, target):
        copy = pltpu.make_async_remote_copy(
            src_ref=src, dst_ref=dst, send_sem=send_sem.at[len(sent)],
            recv_sem=event(name), device_id=target, device_id_type=MESH,
        )
        copy.start()
        sent.append(copy)

    def arrived(name, dst):
        pltpu.make_async_remote_copy(
            src_ref=dst, dst_ref=dst, send_sem=send_sem.at[0],
            recv_sem=event(name), device_id=sibling, device_id_type=MESH,
        ).wait_recv()

    wide = COLS // GROUPS
    loads = []
    for g in range(GROUPS):
        cols = pl.ds(g * wide, wide)
        copy = pltpu.make_async_copy(cot_hbm.at[:, cols], cot.at[:, cols], load_sem.at[g])
        copy.start()
        loads.append(copy)
    barrier = pltpu.get_barrier_semaphore()
    partners = (
        [at_8(k) for k in range(1, 8)]
        + [at_y(k) for k in range(1, NY)]
        + [at_z(k) for k in range(1, NZ)]
    )
    for partner in partners:
        pl.semaphore_signal(barrier, inc=1, device_id=partner, device_id_type=MESH)

    for q in range(4):
        ubuf[q, y, zl] = up[:, q * QUART:(q + 1) * QUART]
        for i in range(LAT // BLOCK):
            for j in range(QUART // BLOCK):
                col = q * QUART + j * BLOCK
                block = quant[i * BLOCK:(i + 1) * BLOCK, col:col + BLOCK].astype(jnp.float32)
                wbuf[q, y, zl, i * BLOCK:(i + 1) * BLOCK, j * BLOCK:(j + 1) * BLOCK] = (
                    block * scales[i, col // BLOCK]
                ).astype(jnp.bfloat16)
    pl.semaphore_wait(barrier, len(partners))

    def slot(j, da, db):
        dy, dz = (da, db) if j == 0 else (db, da)
        return lax.rem(y + dy + NY, NY), lax.rem(zl + dz + NS, NS)

    def along(j, axis, step):
        return at_y(step) if (j == 0) == (axis == 0) else at_z(step)

    def up_ref(j, da, db, core=None):
        ys, zs = slot(j, da, db)
        return ubuf.at[2 * (c if core is None else core) + j, ys, zs]

    def w_ref(j, da, db, part="fetch", core=None):
        ys, zs = slot(j, da, db)
        ref = wbuf.at[2 * (c if core is None else core) + j, ys, zs]
        low = par * EXCL
        if part == "fetch":
            return ref.at[pl.ds(low, FETCH)]
        if part == "h0":
            return ref.at[pl.ds(low, FETCH // 2)]
        if part == "h1":
            return ref.at[pl.ds(low + FETCH // 2, FETCH // 2)]
        if part == "mine":
            return ref.at[pl.ds(par * FETCH, EXCL)]
        if part == "missing":
            return ref.at[pl.ds((1 - par) * FETCH, EXCL)]
        return ref

    def pass_up(j, da):
        for step, name in ((1, -1), (-1, 1), (2, 2)):
            ref = up_ref(j, da, 0)
            send(("u", j, da, name), ref, ref, along(j, 1, step))

    def up_start():
        for j in (0, 1):
            own_up = up_ref(j, 0, 0)
            for step, name in ((1, -1), (-1, 1), (2, 2)):
                send(("u", j, name, 0), own_up, own_up, along(j, 0, step))
        for j in (0, 1):
            pass_up(j, 0)

    def up_first(da):
        for j in (0, 1):
            arrived(("u", j, da, 0), up_ref(j, da, 0))
            pass_up(j, da)

    def up_share():
        for j in (0, 1):
            for da in (0, -1, 1, 2):
                for db in (-1, 1, 2):
                    arrived(("u", j, da, db), up_ref(j, da, db))
            ref = ubuf.at[2 * c + j]
            send(("us", j), ref, ref, sibling)

    def up_finish():
        for j in (0, 1):
            arrived(("us", j), ubuf.at[2 * (1 - c) + j])

    def w_second(j, da):
        ref = w_ref(j, da, 0)
        send(("w", j, da, -1), ref, ref, along(j, 1, 1))
        send(("w", j, da, 1), ref, ref, along(j, 1, -1))

    def w_start():
        for j in (0, 1):
            ref = w_ref(j, 0, 0)
            send(("w", j, -1, 0), ref, ref, along(j, 0, 1))
            send(("w", j, 1, 0), ref, ref, along(j, 0, -1))
        for j in (0, 1):
            w_second(j, 0)

    def w_take(j, da, db):
        if 2 in (da, db) and (db == 2 or db == 0):
            arrived(("w", j, da, db, 0), w_ref(j, da, db, "h0"))
            arrived(("w", j, da, db, 1), w_ref(j, da, db, "h1"))
        else:
            arrived(("w", j, da, db), w_ref(j, da, db))
        axis, o = (0, da) if db == 0 else (1, db)
        if o in (-1, 1):
            ref = w_ref(j, da, db, "h0" if o == -1 else "h1")
            name = ("w", j, 2, 0) if axis == 0 else ("w", j, da, 2)
            send(name + (0 if o == -1 else 1,), ref, ref, along(j, axis, -o))
        if db == 0:
            w_second(j, da)
        ref = w_ref(j, da, db, "mine")
        send(("wx", j, da, db), ref, ref, at_x(1 if j == 0 else -1))

    def w_share(j, da, db):
        arrived(("wx", j, da, db), w_ref(j, da, db, "missing"))
        ref = w_ref(j, da, db, "all")
        send(("ws", j, da, db), ref, ref, sibling)

    def w_use(j, da, db, wait=True):
        if wait:
            arrived(("ws", j, da, db), w_ref(j, da, db, "all", 1 - c))
        ys, zs = slot(j, da, db)
        total = None
        for core in (0, 1):
            q = 2 * core + j
            base = pl.multiple_of((ys * NS + zs) * SHARD + q * QUART, QUART)
            term = dot_cols(cot[:, pl.ds(base, QUART)], wbuf[q, ys, zs])
            total = term if total is None else total + term
        acc[...] += total

    def b_terms(g):
        loads[g].wait()
        for s in range(g * GROUPS, (g + 1) * GROUPS):
            term = jnp.dot(
                low_t[...], cot[:, s * SHARD:(s + 1) * SHARD],
                preferred_element_type=jnp.float32,
            )
            own[s] = jnp.where(c == 0, term[:HALF], term[HALF:])
            sib_out[s] = jnp.where(c == 0, term[HALF:], term[:HALF]).astype(jnp.bfloat16)
        part = pl.ds(g * GROUPS, GROUPS)
        send(("b0", g), sib_out.at[part], sib_in.at[part], sibling)

    def b_cores(g):
        part = pl.ds(g * GROUPS, GROUPS)
        arrived(("b0", g), sib_in.at[part])
        for s in range(g * GROUPS, (g + 1) * GROUPS):
            total = own[s] + sib_in[s].astype(jnp.float32)
            own[s] = total
            for k in range(NX):
                x_out[k, s] = total[:, k * QUART:(k + 1) * QUART].astype(jnp.bfloat16)

    def b_x_send():
        for k in (1, 3, 2):
            send(("b1", k), x_out.at[lax.rem(x + k, NX)], x_in.at[k - 1], at_x(k))

    def b_x_sum():
        for k in (1, 3, 2):
            arrived(("b1", k), x_in.at[k - 1])
        mine = pl.ds(pl.multiple_of(x * QUART, QUART), QUART)
        for yy in range(NY):
            for zz in range(NS):
                s = yy * NS + zz
                total = own[s, :, mine]
                for k in range(NX - 1):
                    total = total + x_in[k, s].astype(jnp.float32)
                y_own[yy, zz] = total
        for k in (1, 3, 2):
            send(("b2", k), y_own.at[lax.rem(y + k, NY)], y_in.at[k - 1], at_y(k))

    def b_y_sum():
        for k in (1, 3, 2):
            arrived(("b2", k), y_in.at[k - 1])
        for zz in range(NS):
            total = y_own[y, zz]
            for k in range(NY - 1):
                total = total + y_in[k, zz]
            z_own[zz] = total
        z_in[z] = z_own[zl]
        for k in range(1, NZ):
            send(("b3", k), z_own.at[lax.rem(zl + k, NS)], z_in.at[z], at_z(k))

    def b_z_sum():
        for k in range(1, NZ):
            arrived(("b3", k), z_in.at[lax.rem(z + NZ - k, NZ)])
        total = z_in[0]
        for k in range(1, NZ):
            total = total + z_in[k]
        gath[me8] = total * (1.0 / TOTAL ** 0.5)
        for k in range(1, 8):
            send(("b4", k), gath.at[me8], gath.at[me8], at_8(k))

    def b_write():
        for k in range(1, 8):
            arrived(("b4", k), gath.at[lax.rem(me8 + 8 - k, 8)])
        for p in range(8):
            rows, cols = (p % 2) * HALF, (p // 2) * QUART
            out_b[rows:rows + HALF, cols:cols + QUART] = gath[p]

    def a_terms():
        def step(s, total):
            for q in range(4):
                base = pl.multiple_of(s * SHARD + q * QUART, QUART)
                total = total + dot_cols(
                    cot[:, pl.ds(base, QUART)], ubuf[q, lax.div(s, NS), lax.rem(s, NS)]
                )
            return total

        through = lax.fori_loop(0, NY * NS, step, jnp.zeros((TOK, RANK), jnp.float32))
        thr[...] = through.astype(jnp.bfloat16)
        through_t = through.astype(jnp.bfloat16).astype(jnp.float32).T.astype(jnp.bfloat16)
        term = jnp.dot(through_t, latent[...], preferred_element_type=jnp.float32)
        for p in range(8):
            a_own[p] = term[p * 8:(p + 1) * 8]
        for k in range(1, 8):
            send(("a1", k), a_own.at[lax.rem(me8 + k, 8)], a_in.at[k - 1], at_8(k))

    def a_8_sum():
        for k in range(1, 8):
            arrived(("a1", k), a_in.at[k - 1])
        total = a_own[me8]
        for k in range(7):
            total = total + a_in[k]
        for yy in range(NY):
            ay_own[yy] = total[:, yy * BLOCK:(yy + 1) * BLOCK]
        for k in (1, 3, 2):
            send(("a2", k), ay_own.at[lax.rem(y + k, NY)], ay_in.at[k - 1], at_y(k))

    def a_y_sum():
        for k in (1, 3, 2):
            arrived(("a2", k), ay_in.at[k - 1])
        total = ay_own[y]
        for k in range(NY - 1):
            total = total + ay_in[k]
        az_in[z] = total
        for k in range(1, NZ):
            send(("a3", k), az_in.at[z], az_in.at[z], at_z(k))

    def a_z_sum():
        for k in range(1, NZ):
            arrived(("a3", k), az_in.at[lax.rem(z + NZ - k, NZ)])
        total = az_in[0]
        for k in range(1, NZ):
            total = total + az_in[k]
        ay_all[y] = total * (1.0 / TOTAL ** 0.5)
        for k in (1, 3, 2):
            send(("a4", k), ay_all.at[y], ay_all.at[y], at_y(k))

    def a_spread():
        for k in (1, 3, 2):
            arrived(("a4", k), ay_all.at[lax.rem(y + NY - k, NY)])
        for yy in range(NY):
            a_all[me8, :, yy * BLOCK:(yy + 1) * BLOCK] = ay_all[yy]
        for k in range(1, 8):
            send(("a5", k), a_all.at[me8], a_all.at[me8], at_8(k))

    def a_write():
        for k in range(1, 8):
            arrived(("a5", k), a_all.at[lax.rem(me8 + 8 - k, 8)])
        for p in range(8):
            out_a[p * 8:(p + 1) * 8] = a_all[p]

    up_start()
    w_start()
    acc[...] = jnp.zeros_like(acc)
    low = jnp.dot(latent[...], down[...], preferred_element_type=jnp.float32)
    low_t[...] = low.astype(jnp.bfloat16).astype(jnp.float32).T.astype(jnp.bfloat16)
    b_terms(0)
    up_first(-1)
    up_first(1)
    b_terms(1)
    up_first(2)
    b_terms(2)
    b_cores(0)
    b_terms(3)
    for g in range(1, GROUPS):
        b_cores(g)
    b_x_send()

    items = [(j, da, db) for da, db in ORDER for j in (0, 1)]
    extra = {
        0: [lambda: w_use(0, 0, 0, False), lambda: w_use(1, 0, 0, False)],
        4: [up_share],
        8: [up_finish, a_terms],
        11: [b_x_sum],
        14: [a_8_sum],
        16: [b_y_sum],
        18: [a_y_sum],
        20: [b_z_sum],
        23: [a_z_sum],
        27: [a_spread],
        28: [b_write],
    }
    lag_x, lag_s = 3, 6
    for i in range(len(items) + lag_s):
        if i < len(items):
            w_take(*items[i])
        if 0 <= i - lag_x < len(items):
            w_share(*items[i - lag_x])
        if 0 <= i - lag_s < len(items):
            w_use(*items[i - lag_s])
        for task in extra.get(i, ()):
            task()
    out_lat[...] = (acc[...] + dot_cols(thr[...], down[...])).astype(jnp.bfloat16)
    a_write()
    for copy in sent:
        copy.wait_send()


def shards(latent, cotangent, quant, scales, adapter_down, adapter_up):
    vmem = pl.BlockSpec(memory_space=pltpu.VMEM)
    bf16, f32 = jnp.bfloat16, jnp.float32
    lat, grad_a_t, grad_b = pl.pallas_call(
        kernel,
        name="adapter_backward",
        out_shape=(
            jax.ShapeDtypeStruct((TOK, LAT), bf16),
            jax.ShapeDtypeStruct((RANK, LAT), f32),
            jax.ShapeDtypeStruct((RANK, SHARD), f32),
        ),
        in_specs=[
            pl.BlockSpec(memory_space=pltpu.SMEM), vmem,
            pl.BlockSpec(memory_space=pl.ANY), vmem, vmem, vmem,
        ],
        out_specs=(vmem, vmem, vmem),
        scratch_shapes=[
            pltpu.VMEM((TOK, COLS), bf16),
            pltpu.VMEM((4, NY, NS, LAT, QUART), bf16),
            pltpu.VMEM((4, NY, NS, RANK, QUART), bf16),
            pltpu.VMEM((RANK, TOK), bf16),
            pltpu.VMEM((TOK, LAT), f32),
            pltpu.VMEM((TOK, RANK), bf16),
            pltpu.VMEM((NY * NS, HALF, SHARD), f32),
            pltpu.VMEM((NY * NS, HALF, SHARD), bf16),
            pltpu.VMEM((NY * NS, HALF, SHARD), bf16),
            pltpu.VMEM((NX, NY * NS, HALF, QUART), bf16),
            pltpu.VMEM((NX - 1, NY * NS, HALF, QUART), bf16),
            pltpu.VMEM((NY, NS, HALF, QUART), f32),
            pltpu.VMEM((NY - 1, NS, HALF, QUART), f32),
            pltpu.VMEM((NS, HALF, QUART), f32),
            pltpu.VMEM((NZ, HALF, QUART), f32),
            pltpu.VMEM((8, HALF, QUART), f32),
            pltpu.VMEM((8, 8, LAT), f32),
            pltpu.VMEM((7, 8, LAT), f32),
            pltpu.VMEM((NY, 8, BLOCK), f32),
            pltpu.VMEM((NY - 1, 8, BLOCK), f32),
            pltpu.VMEM((NZ, 8, BLOCK), f32),
            pltpu.VMEM((NY, 8, BLOCK), f32),
            pltpu.VMEM((8, 8, LAT), f32),
            pltpu.SemaphoreType.DMA((GROUPS,)),
            pltpu.SemaphoreType.DMA((SENDS,)),
            pltpu.SemaphoreType.DMA((RECVS,)),
        ],
        compiler_params=pltpu.CompilerParams(
            collective_id=0, has_side_effects=True, vmem_limit_bytes=56 * 2**20
        ),
        cost_estimate=pl.CostEstimate(
            flops=2 * TOK * COLS * (LAT + 2 * RANK), bytes_accessed=12 * 2**20, transcendentals=0
        ),
    )(scales, latent, cotangent, quant, adapter_down, adapter_up)
    return lat, grad_a_t.T, grad_b


def solution(mesh):
    placed = (
        P(("dp", "fsdp"), None),
        P(("dp", "fsdp"), None),
        P(None, "fsdp"),
        P(None, "fsdp"),
        P(),
        P(None, "fsdp"),
    )
    return jax.shard_map(
        shards,
        mesh=mesh,
        in_specs=placed,
        out_specs=(P(("dp", "fsdp"), None), P(), P(None, "fsdp")),
        check_vma=False,
    )
```

```python
import jax
import jax.numpy as jnp
from jax import lax
from jax.experimental import pallas as pl
from jax.experimental.pallas import tpu as pltpu
from jax.sharding import PartitionSpec as P

MESH = pl.DeviceIdType.MESH
BLOCK = 128
NX, NY, NZ = 4, 4, 8
NS = 4
TOK, COLS, LAT, RANK = 256, 16384, 512, 64
SHARD = COLS // (NY * NS)
CORE = SHARD // 2
UNIT = CORE // 2
SHARDS = NY * NS
MINE = COLS // 2
CHIP = 2 * TOK
PIECE = RANK // NX
EXCL = 144
FETCH = LAT - EXCL
HALF0 = FETCH // 32 * 16
FACTOR = 1.0 / 65536.0 ** 0.5
SENDS = 192
RECVS = 192

ORDER = [
    (-1, 0), (1, 0), (0, -1), (0, 1), (2, 0),
    (-1, -1), (-1, 1), (1, -1), (1, 1),
    (0, 2), (2, -1), (2, 1), (-1, 2), (1, 2), (2, 2),
]


def dot_cols(left, right):
    return lax.dot_general(
        left, right, (((1,), (1,)), ((), ())), preferred_element_type=jnp.float32
    )


def kernel(
    scales, latent_hbm, cot_hbm, quant_hbm, down_hbm, up_hbm,
    out_lat, out_a, out_b,
    latent, down, quant, cot, wbuf, ubuf, low_t, acc, acc_in, thr, thr_in, own, x_out, x_in,
    y_own, y_out, y_in, z_own, z_in, gath,
    a_own, a_in, ay_in, az_in, a_all,
    load_sem, send_sem, recv_sem,
):
    d, f = lax.axis_index("dp"), lax.axis_index("fsdp")
    x, c = lax.div(d, 4), lax.rem(d, 2)
    y, zl = lax.div(f, 4), lax.rem(f, 4)
    z = lax.rem(lax.div(d, 2), 2) * 4 + zl
    par = lax.rem(x, 2)
    me8 = x * 2 + c

    def dev(xx, yy, zz, cc):
        return (xx * 4 + lax.div(zz, 4) * 2 + cc, yy * 4 + lax.rem(zz, 4))

    def at_x(k):
        return dev(lax.rem(x + k + NX, NX), y, z, c)

    def at_y(k):
        return dev(x, lax.rem(y + k + NY, NY), z, c)

    def at_z(k):
        return dev(x, y, lax.rem(z + k + NZ, NZ), c)

    def at_8(k):
        p = lax.rem(me8 + k, 8)
        return dev(lax.div(p, 2), y, z, lax.rem(p, 2))

    sibling = dev(x, y, z, 1 - c)

    sent = []
    events = {}

    def event(name):
        return recv_sem.at[events.setdefault(name, len(events))]

    def send(name, src, dst, target):
        copy = pltpu.make_async_remote_copy(
            src_ref=src, dst_ref=dst, send_sem=send_sem.at[len(sent)],
            recv_sem=event(name), device_id=target, device_id_type=MESH,
        )
        copy.start()
        sent.append(copy)

    def arrived(name, dst):
        pltpu.make_async_remote_copy(
            src_ref=dst, dst_ref=dst, send_sem=send_sem.at[0],
            recv_sem=event(name), device_id=sibling, device_id_type=MESH,
        ).wait_recv()

    barrier = pltpu.get_barrier_semaphore()
    partners = (
        [at_8(k) for k in range(1, 8)]
        + [at_y(k) for k in range(1, NY)]
        + [at_z(k) for k in range(1, NZ)]
    )
    for partner in partners:
        pl.semaphore_signal(barrier, inc=1, device_id=partner, device_id_type=MESH)

    loads = {}

    def load(name, src, dst):
        copy = pltpu.make_async_copy(src, dst, load_sem.at[len(loads)])
        copy.start()
        loads[name] = copy

    half = pl.multiple_of(c * CORE, CORE)
    tokens = pl.ds(pl.multiple_of(c * TOK, TOK), TOK)
    others = pl.ds(pl.multiple_of((1 - c) * TOK, TOK), TOK)
    for j in (0, 1):
        load(("up", j), up_hbm.at[:, pl.ds(half + j * UNIT, UNIT)], ubuf.at[j, y, zl])
    load("quant", quant_hbm.at[:, pl.ds(half, CORE)], quant)
    load("latent", latent_hbm, latent)
    load("down", down_hbm, down)
    for s in range(SHARDS):
        load(
            ("cot", s), cot_hbm.at[:, pl.ds(s * SHARD + half, CORE)],
            cot.at[tokens, pl.ds(s * CORE, CORE)],
        )

    def slot(j, da, db):
        dy, dz = (da, db) if j == 0 else (db, da)
        return lax.rem(y + dy + NY, NY), lax.rem(zl + dz + NS, NS)

    def along(j, axis, step):
        return at_y(step) if (j == 0) == (axis == 0) else at_z(step)

    def up_ref(j, da, db):
        ys, zs = slot(j, da, db)
        return ubuf.at[j, ys, zs]

    def w_ref(j, da, db, part="fetch"):
        ys, zs = slot(j, da, db)
        ref = wbuf.at[j, ys, zs]
        low = par * EXCL
        if part == "fetch":
            return ref.at[pl.ds(low, FETCH)]
        if part == "h0":
            return ref.at[pl.ds(low, HALF0)]
        if part == "h1":
            return ref.at[pl.ds(low + HALF0, FETCH - HALF0)]
        if part == "mine":
            return ref.at[pl.ds(par * FETCH, EXCL)]
        return ref.at[pl.ds((1 - par) * FETCH, EXCL)]

    def pass_up(j, da):
        for step, name in ((1, -1), (-1, 1), (2, 2)):
            ref = up_ref(j, da, 0)
            send(("u", j, da, name), ref, ref, along(j, 1, step))

    def up_start():
        for j in (0, 1):
            own_up = up_ref(j, 0, 0)
            for step, name in ((1, -1), (-1, 1), (2, 2)):
                send(("u", j, name, 0), own_up, own_up, along(j, 0, step))
        for j in (0, 1):
            pass_up(j, 0)

    def up_first(da):
        for j in (0, 1):
            arrived(("u", j, da, 0), up_ref(j, da, 0))
            pass_up(j, da)

    def up_all():
        for j in (0, 1):
            for da in (0, -1, 1, 2):
                for db in (-1, 1, 2):
                    arrived(("u", j, da, db), up_ref(j, da, db))

    def w_second(j, da):
        ref = w_ref(j, da, 0)
        send(("w", j, da, -1), ref, ref, along(j, 1, 1))
        send(("w", j, da, 1), ref, ref, along(j, 1, -1))

    def w_start(j):
        for i in range(LAT // BLOCK):
            for k in range(UNIT // BLOCK):
                col = j * UNIT + k * BLOCK
                block = quant[i * BLOCK:(i + 1) * BLOCK, col:col + BLOCK].astype(jnp.float32)
                wbuf[j, y, zl, i * BLOCK:(i + 1) * BLOCK, k * BLOCK:(k + 1) * BLOCK] = (
                    block * scales[i, c * (CORE // BLOCK) + col // BLOCK]
                ).astype(jnp.bfloat16)
        ref = w_ref(j, 0, 0)
        send(("w", j, -1, 0), ref, ref, along(j, 0, 1))
        send(("w", j, 1, 0), ref, ref, along(j, 0, -1))

    def w_take(j, da, db):
        if db == 2 or (da, db) == (2, 0):
            arrived(("w", j, da, db, 0), w_ref(j, da, db, "h0"))
            arrived(("w", j, da, db, 1), w_ref(j, da, db, "h1"))
        else:
            arrived(("w", j, da, db), w_ref(j, da, db))
        axis, o = (0, da) if db == 0 else (1, db)
        if o in (-1, 1):
            ref = w_ref(j, da, db, "h0" if o == -1 else "h1")
            name = ("w", j, 2, 0) if axis == 0 else ("w", j, da, 2)
            send(name + (0 if o == -1 else 1,), ref, ref, along(j, axis, -o))
        ref = w_ref(j, da, db, "mine")
        send(("wx", j, da, db), ref, ref, at_x(1 if j == 0 else -1))

    def w_ready(da, db):
        for j in (0, 1):
            arrived(("wx", j, da, db), w_ref(j, da, db, "missing"))

    def w_use(da, db, rows=slice(None)):
        total = None
        for j in (0, 1):
            ys, zs = slot(j, da, db)
            base = pl.multiple_of((ys * NS + zs) * CORE + j * UNIT, UNIT)
            term = dot_cols(cot[rows, pl.ds(base, UNIT)], wbuf[j, ys, zs])
            total = term if total is None else total + term
        if (da, db) == (0, 0):
            acc[...] = total
        else:
            acc[rows] += total

    def low_start():
        loads["latent"].wait()
        loads["down"].wait()
        low = jnp.dot(
            latent[...], down[...].astype(jnp.float32).T.astype(jnp.bfloat16),
            preferred_element_type=jnp.float32,
        )
        low_t[c] = low.astype(jnp.bfloat16).astype(jnp.float32).T.astype(jnp.bfloat16)
        send("low", low_t.at[c], low_t.at[c], sibling)

    def cot_send():
        for s in range(SHARDS):
            send(
                ("cot", s), cot_hbm.at[:, pl.ds(s * SHARD + CORE - half, CORE)],
                cot.at[tokens, pl.ds(s * CORE, CORE)], sibling,
            )

    def cot_wait(s):
        loads["cot", s].wait()
        arrived(("cot", s), cot.at[others, pl.ds(s * CORE, CORE)])

    def b_terms(g):
        if g == 0:
            arrived("low", low_t.at[1 - c])
        for s in range(g * NS, (g + 1) * NS):
            cot_wait(s)
            cols = slice(s * CORE, (s + 1) * CORE)
            term = jnp.dot(low_t[0], cot[:TOK, cols], preferred_element_type=jnp.float32)
            term += jnp.dot(low_t[1], cot[TOK:, cols], preferred_element_type=jnp.float32)
            own[s] = term
            for k in range(NX):
                x_out[k, s] = term[k * PIECE:(k + 1) * PIECE].astype(jnp.bfloat16)
        part = pl.ds(g * NS, NS)
        for k in (1, 3, 2):
            send(
                ("b1", k, g), x_out.at[lax.rem(x + k, NX), part], x_in.at[k - 1, part], at_x(k)
            )

    def b_x_sum():
        mine = pl.ds(pl.multiple_of(x * PIECE, PIECE), PIECE)
        for g in range(NY):
            for k in (1, 3, 2):
                arrived(("b1", k, g), x_in.at[k - 1, pl.ds(g * NS, NS)])
            for zz in range(NS):
                s = g * NS + zz
                total = own[s, mine]
                for k in range(NX - 1):
                    total = total + x_in[k, s].astype(jnp.float32)
                y_own[g, zz] = total
                y_out[g, zz] = total.astype(jnp.bfloat16)
        for k in (1, 3, 2):
            send(("b2", k), y_out.at[lax.rem(y + k, NY)], y_in.at[k - 1], at_y(k))

    def b_y_sum():
        for k in (1, 3, 2):
            arrived(("b2", k), y_in.at[k - 1])
        for zz in range(NS):
            total = y_own[y, zz]
            for k in range(NY - 1):
                total = total + y_in[k, zz].astype(jnp.float32)
            z_own[zz] = total
        z_in[z] = z_own[zl]
        for k in range(1, NZ):
            send(("b3", k), z_own.at[lax.rem(zl + k, NS)], z_in.at[z], at_z(k))

    def b_z_sum():
        for k in range(1, NZ):
            arrived(("b3", k), z_in.at[lax.rem(z + NZ - k, NZ)])
        total = z_in[0]
        for k in range(1, NZ):
            total = total + z_in[k]
        gath[me8] = total * FACTOR
        for k in range(1, 8):
            send(("b4", k), gath.at[me8], gath.at[me8], at_8(k))

    def b_write():
        for k in range(1, 8):
            arrived(("b4", k), gath.at[lax.rem(me8 + 8 - k, 8)])
        for p in range(8):
            rows, cols = (p // 2) * PIECE, (p % 2) * CORE
            out_b[rows:rows + PIECE, cols:cols + CORE] = gath[p]

    def a_through():
        def step(s, total):
            for j in (0, 1):
                base = pl.multiple_of(s * CORE + j * UNIT, UNIT)
                total = total + dot_cols(
                    cot[:, pl.ds(base, UNIT)], ubuf[j, lax.div(s, NS), lax.rem(s, NS)]
                )
            return total

        through = lax.fori_loop(0, SHARDS, step, jnp.zeros((CHIP, RANK), jnp.float32)).T
        for core in (0, 1):
            thr[core] = through[:, core * TOK:(core + 1) * TOK]
        send("thr", thr.at[1 - c], thr_in, sibling)

    def a_terms():
        arrived("thr", thr_in)
        total = (thr[c] + thr_in[...]).astype(jnp.bfloat16)
        thr[c] = total.astype(jnp.float32)
        term = jnp.dot(total, latent[...], preferred_element_type=jnp.float32)
        for p in range(8):
            a_own[p] = term[p * 8:(p + 1) * 8]
        for k in range(1, 8):
            send(("a1", k), a_own.at[lax.rem(me8 + k, 8)], a_in.at[k - 1], at_8(k))

    def a_8_sum():
        for k in range(1, 8):
            arrived(("a1", k), a_in.at[k - 1])
        total = a_own[me8]
        for k in range(7):
            total = total + a_in[k]
        ay_in[y] = total
        for k in (1, 3, 2):
            send(("a2", k), ay_in.at[y], ay_in.at[y], at_y(k))

    def a_y_sum():
        for k in (1, 3, 2):
            arrived(("a2", k), ay_in.at[lax.rem(y + NY - k, NY)])
        total = ay_in[0]
        for k in range(1, NY):
            total = total + ay_in[k]
        az_in[z] = total
        for k in range(1, NZ):
            send(("a3", k), az_in.at[z], az_in.at[z], at_z(k))

    def a_z_sum():
        for k in range(1, NZ):
            arrived(("a3", k), az_in.at[lax.rem(z + NZ - k, NZ)])
        total = az_in[0]
        for k in range(1, NZ):
            total = total + az_in[k]
        a_all[me8] = total * FACTOR
        for k in range(1, 8):
            send(("a4", k), a_all.at[me8], a_all.at[me8], at_8(k))

    def a_write():
        for k in range(1, 8):
            arrived(("a4", k), a_all.at[lax.rem(me8 + 8 - k, 8)])
        for p in range(8):
            out_a[p * 8:(p + 1) * 8] = a_all[p]

    def up_wait():
        for j in (0, 1):
            loads["up", j].wait()
        pl.semaphore_wait(barrier, len(partners))

    def take(*pairs):
        for da, db in pairs:
            for j in (0, 1):
                w_take(j, da, db)

    def second(da):
        for j in (0, 1):
            w_second(j, da)

    def use(*pairs):
        for pair in pairs:
            w_ready(*pair)
            w_use(*pair)

    def w_first():
        loads["quant"].wait()
        for j in (0, 1):
            w_start(j)

    up_wait()
    up_start()
    cot_send()
    w_first()
    low_start()
    up_first(-1)
    up_first(1)
    up_first(2)
    second(0)
    b_terms(0)
    b_terms(1)
    take((-1, 0), (1, 0))
    second(-1)
    b_terms(2)
    b_terms(3)
    up_all()
    a_through()
    take((0, -1), (0, 1))
    w_use(0, 0)
    a_terms()
    take((2, 0))
    use((-1, 0), (1, 0))
    b_x_sum()
    second(1)
    take((-1, -1), (-1, 1))
    use((0, -1), (0, 1))
    a_8_sum()
    second(2)
    use((2, 0))
    b_y_sum()
    take((0, 2))
    take((1, -1), (1, 1))
    use((-1, -1), (-1, 1))
    a_y_sum()
    take((-1, 2))
    use((0, 2), (1, -1), (1, 1))
    b_z_sum()
    take((2, -1), (2, 1))
    use((-1, 2))
    a_z_sum()
    take((1, 2))
    use((2, -1), (2, 1))
    b_write()
    take((2, 2))
    use((1, 2))
    w_ready(2, 2)
    w_use(2, 2, others)
    send("acc", acc.at[others], acc_in, sibling)
    w_use(2, 2, tokens)
    acc[tokens] += jnp.dot(
        thr[c].T.astype(jnp.bfloat16), down[...], preferred_element_type=jnp.float32
    )
    a_write()
    arrived("acc", acc_in)
    out_lat[...] = (acc[tokens] + acc_in[...]).astype(jnp.bfloat16)
    for copy in sent:
        copy.wait_send()


def tidy(lat, grad_a, grad_b, out_lat, out_a, out_b):
    out_lat[...] = lat[...]
    out_a[...] = grad_a[...]
    out_b[...] = grad_b[...]


def shards(latent, cotangent, quant, scales, adapter_down, adapter_up):
    vmem = pl.BlockSpec(memory_space=pltpu.VMEM)
    hbm = pl.BlockSpec(memory_space=pl.ANY)
    bf16, f32 = jnp.bfloat16, jnp.float32
    results = (
        jax.ShapeDtypeStruct((TOK, LAT), bf16),
        jax.ShapeDtypeStruct((RANK, LAT), f32),
        jax.ShapeDtypeStruct((RANK, SHARD), f32),
    )
    outs = pl.pallas_call(
        kernel,
        name="adapter_backward",
        out_shape=results,
        in_specs=[pl.BlockSpec(memory_space=pltpu.SMEM)] + [hbm] * 5,
        out_specs=(vmem, vmem, vmem),
        scratch_shapes=[
            pltpu.VMEM((TOK, LAT), bf16),
            pltpu.VMEM((RANK, LAT), bf16),
            pltpu.VMEM((LAT, CORE), bf16),
            pltpu.VMEM((CHIP, MINE), bf16),
            pltpu.VMEM((2, NY, NS, LAT, UNIT), bf16),
            pltpu.VMEM((2, NY, NS, RANK, UNIT), bf16),
            pltpu.VMEM((2, RANK, TOK), bf16),
            pltpu.VMEM((CHIP, LAT), f32),
            pltpu.VMEM((TOK, LAT), f32),
            pltpu.VMEM((2, RANK, TOK), f32),
            pltpu.VMEM((RANK, TOK), f32),
            pltpu.VMEM((SHARDS, RANK, CORE), f32),
            pltpu.VMEM((NX, SHARDS, PIECE, CORE), bf16),
            pltpu.VMEM((NX - 1, SHARDS, PIECE, CORE), bf16),
            pltpu.VMEM((NY, NS, PIECE, CORE), f32),
            pltpu.VMEM((NY, NS, PIECE, CORE), bf16),
            pltpu.VMEM((NY - 1, NS, PIECE, CORE), bf16),
            pltpu.VMEM((NS, PIECE, CORE), f32),
            pltpu.VMEM((NZ, PIECE, CORE), f32),
            pltpu.VMEM((8, PIECE, CORE), f32),
            pltpu.VMEM((8, 8, LAT), f32),
            pltpu.VMEM((7, 8, LAT), f32),
            pltpu.VMEM((NY, 8, LAT), f32),
            pltpu.VMEM((NZ, 8, LAT), f32),
            pltpu.VMEM((8, 8, LAT), f32),
            pltpu.SemaphoreType.DMA((5 + SHARDS,)),
            pltpu.SemaphoreType.DMA((SENDS,)),
            pltpu.SemaphoreType.DMA((RECVS,)),
        ],
        compiler_params=pltpu.CompilerParams(
            collective_id=0, has_side_effects=True, vmem_limit_bytes=56 * 2**20
        ),
        cost_estimate=pl.CostEstimate(
            flops=2 * TOK * COLS * (LAT + 2 * RANK), bytes_accessed=12 * 2**20, transcendentals=0
        ),
    )(scales, latent, cotangent, quant, adapter_down.T, adapter_up)
    lat, grad_a_t, grad_b = pl.pallas_call(
        tidy,
        name="tidy",
        out_shape=results,
        in_specs=[vmem] * 3,
        out_specs=(vmem, vmem, vmem),
    )(*outs)
    return lat, grad_a_t.T, grad_b


def solution(mesh):
    placed = (
        P(("dp", "fsdp"), None),
        P(("dp", "fsdp"), None),
        P(None, "fsdp"),
        P(None, "fsdp"),
        P(),
        P(None, "fsdp"),
    )
    return jax.shard_map(
        shards,
        mesh=mesh,
        in_specs=placed,
        out_specs=(P(("dp", "fsdp"), None), P(), P(None, "fsdp")),
        check_vma=False,
    )
```

```python
import jax
import jax.numpy as jnp
from jax import lax
from jax.experimental import pallas as pl
from jax.experimental.pallas import tpu as pltpu
from jax.sharding import PartitionSpec as P

MESH = pl.DeviceIdType.MESH
BLOCK = 128
NX, NY, NZ = 4, 4, 8
NS = 4
TOK, COLS, LAT, RANK = 256, 16384, 512, 64
SHARD = COLS // (NY * NS)
CORE = SHARD // 2
UNIT = CORE // 2
SHARDS = NY * NS
MINE = COLS // 2
CHIP = 2 * TOK
PIECE = RANK // NX
EXCL = 144
FETCH = LAT - EXCL
HALF0 = FETCH // 32 * 16
FACTOR = 1.0 / 65536.0 ** 0.5
SENDS = 208
RECVS = 208

ORDER = [
    (-1, 0), (1, 0), (0, -1), (0, 1), (2, 0),
    (-1, -1), (-1, 1), (1, -1), (1, 1),
    (0, 2), (2, -1), (2, 1), (-1, 2), (1, 2), (2, 2),
]


def dot_cols(left, right):
    return lax.dot_general(
        left, right, (((1,), (1,)), ((), ())), preferred_element_type=jnp.float32
    )


def kernel(
    scales, latent_hbm, cot_hbm, quant_hbm, down_hbm, up_hbm,
    out_lat, out_a, out_b,
    latent, down, quant, cot, wbuf, ubuf, low_t, acc, acc_in, thr, thr_in, own, x_out, x_in,
    y_own, y_out, y_in, z_own, z_in, gath,
    a_own, a_in, ay_in, az_in, a_all,
    load_sem, send_sem, recv_sem,
):
    d, f = lax.axis_index("dp"), lax.axis_index("fsdp")
    x, c = lax.div(d, 4), lax.rem(d, 2)
    y, zl = lax.div(f, 4), lax.rem(f, 4)
    z = lax.rem(lax.div(d, 2), 2) * 4 + zl
    par = lax.rem(x, 2)
    me8 = x * 2 + c

    def dev(xx, yy, zz, cc):
        return (xx * 4 + lax.div(zz, 4) * 2 + cc, yy * 4 + lax.rem(zz, 4))

    def at_x(k):
        return dev(lax.rem(x + k + NX, NX), y, z, c)

    def at_y(k):
        return dev(x, lax.rem(y + k + NY, NY), z, c)

    def at_z(k):
        return dev(x, y, lax.rem(z + k + NZ, NZ), c)

    def at_8(k):
        p = lax.rem(me8 + k, 8)
        return dev(lax.div(p, 2), y, z, lax.rem(p, 2))

    sibling = dev(x, y, z, 1 - c)

    sent = []
    events = {}

    def event(name):
        return recv_sem.at[events.setdefault(name, len(events))]

    def send(name, src, dst, target):
        copy = pltpu.make_async_remote_copy(
            src_ref=src, dst_ref=dst, send_sem=send_sem.at[len(sent)],
            recv_sem=event(name), device_id=target, device_id_type=MESH,
        )
        copy.start()
        sent.append(copy)

    def arrived(name, dst):
        pltpu.make_async_remote_copy(
            src_ref=dst, dst_ref=dst, send_sem=send_sem.at[0],
            recv_sem=event(name), device_id=sibling, device_id_type=MESH,
        ).wait_recv()

    barrier = pltpu.get_barrier_semaphore()
    partners = (
        [at_8(k) for k in range(1, 8)]
        + [at_y(k) for k in range(1, NY)]
        + [at_z(k) for k in range(1, NZ)]
    )
    for partner in partners:
        pl.semaphore_signal(barrier, inc=1, device_id=partner, device_id_type=MESH)

    loads = {}

    def load(name, src, dst):
        copy = pltpu.make_async_copy(src, dst, load_sem.at[len(loads)])
        copy.start()
        loads[name] = copy

    half = pl.multiple_of(c * CORE, CORE)
    tokens = pl.ds(pl.multiple_of(c * TOK, TOK), TOK)
    others = pl.ds(pl.multiple_of((1 - c) * TOK, TOK), TOK)
    for j in (0, 1):
        load(("up", j), up_hbm.at[:, pl.ds(half + j * UNIT, UNIT)], ubuf.at[j, y, zl])
    load("quant", quant_hbm.at[:, pl.ds(half, CORE)], quant)
    load("latent", latent_hbm, latent)
    load("down", down_hbm, down)
    for s in range(SHARDS):
        load(
            ("cot", s), cot_hbm.at[:, pl.ds(s * SHARD + half, CORE)],
            cot.at[tokens, pl.ds(s * CORE, CORE)],
        )

    def slot(j, da, db):
        dy, dz = (da, db) if j == 0 else (db, da)
        return lax.rem(y + dy + NY, NY), lax.rem(zl + dz + NS, NS)

    def along(j, axis, step):
        return at_y(step) if (j == 0) == (axis == 0) else at_z(step)

    def up_ref(j, da, db, part=None):
        ys, zs = slot(j, da, db)
        ref = ubuf.at[j, ys, zs]
        return ref if part is None else ref.at[part * (RANK // 2):(part + 1) * (RANK // 2)]

    def w_ref(j, da, db, part="fetch"):
        ys, zs = slot(j, da, db)
        ref = wbuf.at[j, ys, zs]
        low = par * EXCL
        if part == "fetch":
            return ref.at[pl.ds(low, FETCH)]
        if part == "h0":
            return ref.at[pl.ds(low, HALF0)]
        if part == "h1":
            return ref.at[pl.ds(low + HALF0, FETCH - HALF0)]
        if part == "mine":
            return ref.at[pl.ds(par * FETCH, EXCL)]
        return ref.at[pl.ds((1 - par) * FETCH, EXCL)]

    def up_second(j, da):
        ref = up_ref(j, da, 0)
        send(("u", j, da, -1), ref, ref, along(j, 1, 1))
        send(("u", j, da, 1), ref, ref, along(j, 1, -1))

    def up_start():
        for j in (0, 1):
            ref = up_ref(j, 0, 0)
            send(("u", j, -1, 0), ref, ref, along(j, 0, 1))
            send(("u", j, 1, 0), ref, ref, along(j, 0, -1))
        for j in (0, 1):
            up_second(j, 0)

    def up_pass(j, axis, o, da, name):
        part = 0 if o == -1 else 1
        db = 0 if axis == 0 else o
        ref = up_ref(j, da, db, part)
        send(name + (part,), ref, ref, along(j, axis, -o))

    def up_first(o):
        for j in (0, 1):
            arrived(("u", j, o, 0), up_ref(j, o, 0))
            up_pass(j, 0, o, o, ("u", j, 2, 0))
            up_second(j, o)

    def up_far():
        for j in (0, 1):
            for part in (0, 1):
                arrived(("u", j, 2, 0, part), up_ref(j, 2, 0, part))
            up_second(j, 2)

    def up_turn(da):
        for o in (-1, 1):
            for j in (0, 1):
                arrived(("u", j, da, o), up_ref(j, da, o))
                up_pass(j, 1, o, da, ("u", j, da, 2))

    def up_all():
        for da in (0, -1, 1, 2):
            for j in (0, 1):
                for part in (0, 1):
                    arrived(("u", j, da, 2, part), up_ref(j, da, 2, part))

    def w_second(j, da):
        ref = w_ref(j, da, 0)
        send(("w", j, da, -1), ref, ref, along(j, 1, 1))
        send(("w", j, da, 1), ref, ref, along(j, 1, -1))

    def w_start(j):
        for i in range(LAT // BLOCK):
            for k in range(UNIT // BLOCK):
                col = j * UNIT + k * BLOCK
                block = quant[i * BLOCK:(i + 1) * BLOCK, col:col + BLOCK].astype(jnp.float32)
                wbuf[j, y, zl, i * BLOCK:(i + 1) * BLOCK, k * BLOCK:(k + 1) * BLOCK] = (
                    block * scales[i, c * (CORE // BLOCK) + col // BLOCK]
                ).astype(jnp.bfloat16)
        ref = w_ref(j, 0, 0)
        send(("w", j, -1, 0), ref, ref, along(j, 0, 1))
        send(("w", j, 1, 0), ref, ref, along(j, 0, -1))

    def w_take(j, da, db):
        if db == 2 or (da, db) == (2, 0):
            arrived(("w", j, da, db, 0), w_ref(j, da, db, "h0"))
            arrived(("w", j, da, db, 1), w_ref(j, da, db, "h1"))
        else:
            arrived(("w", j, da, db), w_ref(j, da, db))
        axis, o = (0, da) if db == 0 else (1, db)
        if o in (-1, 1):
            ref = w_ref(j, da, db, "h0" if o == -1 else "h1")
            name = ("w", j, 2, 0) if axis == 0 else ("w", j, da, 2)
            send(name + (0 if o == -1 else 1,), ref, ref, along(j, axis, -o))

    def w_cross(j, da, db):
        ref = w_ref(j, da, db, "mine")
        send(("wx", j, da, db), ref, ref, at_x(1 if j == 0 else -1))

    def w_ready(da, db):
        for j in (0, 1):
            arrived(("wx", j, da, db), w_ref(j, da, db, "missing"))

    def w_use(da, db, rows=slice(None)):
        total = None
        for j in (0, 1):
            ys, zs = slot(j, da, db)
            base = pl.multiple_of((ys * NS + zs) * CORE + j * UNIT, UNIT)
            term = dot_cols(cot[rows, pl.ds(base, UNIT)], wbuf[j, ys, zs])
            total = term if total is None else total + term
        if (da, db) == (0, 0):
            acc[...] = total
        else:
            acc[rows] += total

    def low_start():
        loads["latent"].wait()
        loads["down"].wait()
        low = jnp.dot(
            latent[...], down[...].astype(jnp.float32).T.astype(jnp.bfloat16),
            preferred_element_type=jnp.float32,
        )
        low_t[c] = low.astype(jnp.bfloat16).astype(jnp.float32).T.astype(jnp.bfloat16)
        send("low", low_t.at[c], low_t.at[c], sibling)

    def cot_send():
        for s in range(SHARDS):
            send(
                ("cot", s), cot_hbm.at[:, pl.ds(s * SHARD + CORE - half, CORE)],
                cot.at[tokens, pl.ds(s * CORE, CORE)], sibling,
            )

    def cot_wait(s):
        loads["cot", s].wait()
        arrived(("cot", s), cot.at[others, pl.ds(s * CORE, CORE)])

    def b_terms(g):
        if g == 0:
            arrived("low", low_t.at[1 - c])
        for s in range(g * NS, (g + 1) * NS):
            cot_wait(s)
            cols = slice(s * CORE, (s + 1) * CORE)
            term = jnp.dot(low_t[0], cot[:TOK, cols], preferred_element_type=jnp.float32)
            term += jnp.dot(low_t[1], cot[TOK:, cols], preferred_element_type=jnp.float32)
            own[s] = term
            for k in range(NX):
                x_out[k, s] = term[k * PIECE:(k + 1) * PIECE].astype(jnp.bfloat16)
        part = pl.ds(g * NS, NS)
        for k in (1, 3, 2):
            send(
                ("b1", k, g), x_out.at[lax.rem(x + k, NX), part], x_in.at[k - 1, part], at_x(k)
            )

    def b_x_sum():
        mine = pl.ds(pl.multiple_of(x * PIECE, PIECE), PIECE)
        for g in range(NY):
            for k in (1, 3, 2):
                arrived(("b1", k, g), x_in.at[k - 1, pl.ds(g * NS, NS)])
            for zz in range(NS):
                s = g * NS + zz
                total = own[s, mine]
                for k in range(NX - 1):
                    total = total + x_in[k, s].astype(jnp.float32)
                y_own[g, zz] = total
                y_out[g, zz] = total.astype(jnp.bfloat16)
        for k in (1, 3, 2):
            send(("b2", k), y_out.at[lax.rem(y + k, NY)], y_in.at[k - 1], at_y(k))

    def b_y_sum():
        for k in (1, 3, 2):
            arrived(("b2", k), y_in.at[k - 1])
        for zz in range(NS):
            total = y_own[y, zz]
            for k in range(NY - 1):
                total = total + y_in[k, zz].astype(jnp.float32)
            z_own[zz] = total.astype(jnp.bfloat16)
        z_in[z] = z_own[zl]
        for k in range(1, NZ):
            send(("b3", k), z_own.at[lax.rem(zl + k, NS)], z_in.at[z], at_z(k))

    def b_z_sum():
        for k in range(1, NZ):
            arrived(("b3", k), z_in.at[lax.rem(z + NZ - k, NZ)])
        total = z_in[0].astype(jnp.float32)
        for k in range(1, NZ):
            total = total + z_in[k].astype(jnp.float32)
        gath[me8] = total * FACTOR
        for k in range(1, 8):
            send(("b4", k), gath.at[me8], gath.at[me8], at_8(k))

    def b_write():
        for k in range(1, 8):
            arrived(("b4", k), gath.at[lax.rem(me8 + 8 - k, 8)])
        for p in range(8):
            rows, cols = (p // 2) * PIECE, (p % 2) * CORE
            out_b[rows:rows + PIECE, cols:cols + CORE] = gath[p]

    def a_through():
        def step(s, total):
            for j in (0, 1):
                base = pl.multiple_of(s * CORE + j * UNIT, UNIT)
                total = total + dot_cols(
                    ubuf[j, lax.div(s, NS), lax.rem(s, NS)], cot[:, pl.ds(base, UNIT)]
                )
            return total

        through = lax.fori_loop(0, SHARDS, step, jnp.zeros((RANK, CHIP), jnp.float32), unroll=4)
        for core in (0, 1):
            thr[core] = through[:, core * TOK:(core + 1) * TOK]
        send("thr", thr.at[1 - c], thr_in, sibling)

    def a_terms():
        arrived("thr", thr_in)
        total = (thr[c] + thr_in[...]).astype(jnp.bfloat16)
        thr[c] = total.astype(jnp.float32)
        term = jnp.dot(total, latent[...], preferred_element_type=jnp.float32)
        for p in range(8):
            rows, cols = (p // 2) * PIECE, (p % 2) * (LAT // 2)
            a_own[p] = term[rows:rows + PIECE, cols:cols + LAT // 2]
        for k in range(1, 8):
            send(("a1", k), a_own.at[lax.rem(me8 + k, 8)], a_in.at[k - 1], at_8(k))

    def a_8_sum():
        for k in range(1, 8):
            arrived(("a1", k), a_in.at[k - 1])
        total = a_own[me8]
        for k in range(7):
            total = total + a_in[k]
        ay_in[y] = total
        for k in (1, 3, 2):
            send(("a2", k), ay_in.at[y], ay_in.at[y], at_y(k))

    def a_y_sum():
        for k in (1, 3, 2):
            arrived(("a2", k), ay_in.at[lax.rem(y + NY - k, NY)])
        total = ay_in[0]
        for k in range(1, NY):
            total = total + ay_in[k]
        az_in[z] = total.astype(jnp.bfloat16)
        for k in range(1, NZ):
            send(("a3", k), az_in.at[z], az_in.at[z], at_z(k))

    def a_z_sum():
        for k in range(1, NZ):
            arrived(("a3", k), az_in.at[lax.rem(z + NZ - k, NZ)])
        total = az_in[0].astype(jnp.float32)
        for k in range(1, NZ):
            total = total + az_in[k].astype(jnp.float32)
        a_all[me8] = total * FACTOR
        for k in range(1, 8):
            send(("a4", k), a_all.at[me8], a_all.at[me8], at_8(k))

    def a_write():
        for k in range(1, 8):
            arrived(("a4", k), a_all.at[lax.rem(me8 + 8 - k, 8)])
        for p in range(8):
            rows, cols = (p // 2) * PIECE, (p % 2) * (LAT // 2)
            out_a[rows:rows + PIECE, cols:cols + LAT // 2] = a_all[p]

    def up_wait():
        for j in (0, 1):
            loads["up", j].wait()
        pl.semaphore_wait(barrier, len(partners))

    def take(da, db):
        for j in (0, 1):
            w_take(j, da, db)

    def cross(da, db):
        for j in (0, 1):
            w_cross(j, da, db)

    def second(da):
        for j in (0, 1):
            w_second(j, da)

    def use(da, db):
        if (da, db) != (0, 0):
            w_ready(da, db)
        w_use(da, db)

    def w_first():
        loads["quant"].wait()
        for j in (0, 1):
            w_start(j)

    up_wait()
    low_start()
    up_start()
    cot_send()
    w_first()
    second(0)
    up_first(-1)
    b_terms(0)
    take(-1, 0)
    up_first(1)
    take(1, 0)
    cross(-1, 0)
    b_terms(1)
    second(-1)
    take(0, -1)
    b_terms(2)
    cross(0, -1)
    take(0, 1)
    b_terms(3)
    take(2, 0)
    up_far()
    cross(1, 0)
    take(-1, 1)
    up_turn(0)
    take(-1, -1)
    cross(-1, -1)
    up_turn(1)
    take(0, 2)
    up_turn(-1)
    cross(0, 1)
    up_turn(2)
    cross(0, 2)
    second(1)
    cross(2, 0)
    use(0, 0)
    cross(-1, 1)
    b_x_sum()
    second(2)
    take(-1, 2)
    up_all()
    a_through()
    cross(-1, 2)
    a_terms()
    take(1, -1)
    use(0, 1)
    cross(1, -1)
    take(1, 1)
    cross(1, 1)
    b_y_sum()
    use(-1, 2)
    a_8_sum()
    take(2, 1)
    take(2, -1)
    cross(2, 1)
    use(0, 2)
    cross(2, -1)
    use(1, -1)
    take(1, 2)
    cross(1, 2)
    a_y_sum()
    b_z_sum()
    use(2, 0)
    take(2, 2)
    use(0, -1)
    use(-1, 1)
    cross(2, 2)
    use(2, -1)
    use(-1, 0)
    use(2, 1)
    use(1, 1)
    a_z_sum()
    use(1, 2)
    use(-1, -1)
    use(1, 0)
    b_write()
    w_ready(2, 2)
    w_use(2, 2, others)
    send("acc", acc.at[others], acc_in, sibling)
    w_use(2, 2, tokens)
    acc[tokens] += jnp.dot(
        thr[c].T.astype(jnp.bfloat16), down[...], preferred_element_type=jnp.float32
    )
    a_write()
    arrived("acc", acc_in)
    out_lat[...] = (acc[tokens] + acc_in[...]).astype(jnp.bfloat16)
    for copy in sent:
        copy.wait_send()


def tidy(lat, grad_a, grad_b, out_lat, out_a, out_b):
    out_lat[...] = lat[...]
    out_a[...] = grad_a[...]
    out_b[...] = grad_b[...]


def shards(latent, cotangent, quant, scales, adapter_down, adapter_up):
    vmem = pl.BlockSpec(memory_space=pltpu.VMEM)
    hbm = pl.BlockSpec(memory_space=pl.ANY)
    bf16, f32 = jnp.bfloat16, jnp.float32
    results = (
        jax.ShapeDtypeStruct((TOK, LAT), bf16),
        jax.ShapeDtypeStruct((RANK, LAT), f32),
        jax.ShapeDtypeStruct((RANK, SHARD), f32),
    )
    outs = pl.pallas_call(
        kernel,
        name="adapter_backward",
        out_shape=results,
        in_specs=[pl.BlockSpec(memory_space=pltpu.SMEM)] + [hbm] * 5,
        out_specs=(vmem, vmem, vmem),
        scratch_shapes=[
            pltpu.VMEM((TOK, LAT), bf16),
            pltpu.VMEM((RANK, LAT), bf16),
            pltpu.VMEM((LAT, CORE), bf16),
            pltpu.VMEM((CHIP, MINE), bf16),
            pltpu.VMEM((2, NY, NS, LAT, UNIT), bf16),
            pltpu.VMEM((2, NY, NS, RANK, UNIT), bf16),
            pltpu.VMEM((2, RANK, TOK), bf16),
            pltpu.VMEM((CHIP, LAT), f32),
            pltpu.VMEM((TOK, LAT), f32),
            pltpu.VMEM((2, RANK, TOK), f32),
            pltpu.VMEM((RANK, TOK), f32),
            pltpu.VMEM((SHARDS, RANK, CORE), f32),
            pltpu.VMEM((NX, SHARDS, PIECE, CORE), bf16),
            pltpu.VMEM((NX - 1, SHARDS, PIECE, CORE), bf16),
            pltpu.VMEM((NY, NS, PIECE, CORE), f32),
            pltpu.VMEM((NY, NS, PIECE, CORE), bf16),
            pltpu.VMEM((NY - 1, NS, PIECE, CORE), bf16),
            pltpu.VMEM((NS, PIECE, CORE), bf16),
            pltpu.VMEM((NZ, PIECE, CORE), bf16),
            pltpu.VMEM((8, PIECE, CORE), f32),
            pltpu.VMEM((8, PIECE, LAT // 2), f32),
            pltpu.VMEM((7, PIECE, LAT // 2), f32),
            pltpu.VMEM((NY, PIECE, LAT // 2), f32),
            pltpu.VMEM((NZ, PIECE, LAT // 2), bf16),
            pltpu.VMEM((8, PIECE, LAT // 2), f32),
            pltpu.SemaphoreType.DMA((5 + SHARDS,)),
            pltpu.SemaphoreType.DMA((SENDS,)),
            pltpu.SemaphoreType.DMA((RECVS,)),
        ],
        compiler_params=pltpu.CompilerParams(
            collective_id=0, has_side_effects=True, vmem_limit_bytes=56 * 2**20
        ),
        cost_estimate=pl.CostEstimate(
            flops=2 * TOK * COLS * (LAT + 2 * RANK), bytes_accessed=12 * 2**20, transcendentals=0
        ),
    )(scales, latent, cotangent, quant, adapter_down.T, adapter_up)
    lat, grad_a_t, grad_b = pl.pallas_call(
        tidy,
        name="tidy",
        out_shape=results,
        in_specs=[vmem] * 3,
        out_specs=(vmem, vmem, vmem),
    )(*outs)
    return lat, grad_a_t.T, grad_b


def solution(mesh):
    placed = (
        P(("dp", "fsdp"), None),
        P(("dp", "fsdp"), None),
        P(None, "fsdp"),
        P(None, "fsdp"),
        P(),
        P(None, "fsdp"),
    )
    return jax.shard_map(
        shards,
        mesh=mesh,
        in_specs=placed,
        out_specs=(P(("dp", "fsdp"), None), P(), P(None, "fsdp")),
        check_vma=False,
    )
```

```python
import jax
import jax.numpy as jnp
from jax import lax
from jax.experimental import pallas as pl
from jax.experimental.pallas import tpu as pltpu
from jax.sharding import PartitionSpec as P

MESH = pl.DeviceIdType.MESH
BLOCK = 128
NX, NY, NZ = 4, 4, 8
NS = 4
TOK, COLS, LAT, RANK = 256, 16384, 512, 64
SHARD = COLS // (NY * NS)
CORE = SHARD // 2
UNIT = CORE // 2
SHARDS = NY * NS
MINE = COLS // 2
CHIP = 2 * TOK
PIECE = RANK // NX
EXCL = 160
FETCH = LAT - EXCL
HALF0 = FETCH // 32 * 16
FACTOR = 1.0 / 65536.0 ** 0.5
SENDS = 208
RECVS = 208

ORDER = [
    (-1, 0), (1, 0), (0, -1), (0, 1), (2, 0),
    (-1, -1), (-1, 1), (1, -1), (1, 1),
    (0, 2), (2, -1), (2, 1), (-1, 2), (1, 2), (2, 2),
]


def dot_cols(left, right):
    return lax.dot_general(
        left, right, (((1,), (1,)), ((), ())), preferred_element_type=jnp.float32
    )


def kernel(
    scales_hbm, latent_hbm, cot_hbm, quant_hbm, down_hbm, up_hbm,
    out_lat, out_a, out_b,
    latent, down, quant, cot, wbuf, ubuf, low_t, acc, acc_out, acc_in, thr, thr_in, own, x_out, x_in,
    y_own, y_out, y_in, z_own, z_in, gath,
    a_own, a_in, ay_in, az_in, a_all,
    scales, load_sem, send_sem, recv_sem,
):
    d, f = lax.axis_index("dp"), lax.axis_index("fsdp")
    x, c = lax.div(d, 4), lax.rem(d, 2)
    y, zl = lax.div(f, 4), lax.rem(f, 4)
    z = lax.rem(lax.div(d, 2), 2) * 4 + zl
    par = lax.rem(x, 2)
    me8 = x * 2 + c

    def dev(xx, yy, zz, cc):
        return (xx * 4 + lax.div(zz, 4) * 2 + cc, yy * 4 + lax.rem(zz, 4))

    def at_x(k):
        return dev(lax.rem(x + k + NX, NX), y, z, c)

    def at_y(k):
        return dev(x, lax.rem(y + k + NY, NY), z, c)

    def at_z(k):
        return dev(x, y, lax.rem(z + k + NZ, NZ), c)

    def at_8(k):
        p = lax.rem(me8 + k, 8)
        return dev(lax.div(p, 2), y, z, lax.rem(p, 2))

    sibling = dev(x, y, z, 1 - c)

    sent = []
    events = {}

    def event(name):
        return recv_sem.at[events.setdefault(name, len(events))]

    def send(name, src, dst, target):
        copy = pltpu.make_async_remote_copy(
            src_ref=src, dst_ref=dst, send_sem=send_sem.at[len(sent)],
            recv_sem=event(name), device_id=target, device_id_type=MESH,
        )
        copy.start()
        sent.append(copy)

    def arrived(name, dst):
        pltpu.make_async_remote_copy(
            src_ref=dst, dst_ref=dst, send_sem=send_sem.at[0],
            recv_sem=event(name), device_id=sibling, device_id_type=MESH,
        ).wait_recv()

    barrier = pltpu.get_barrier_semaphore()
    partners = (
        [at_8(k) for k in range(1, 8)]
        + [at_y(k) for k in range(1, NY)]
        + [at_z(k) for k in range(1, NZ)]
    )
    for partner in partners:
        pl.semaphore_signal(barrier, inc=1, device_id=partner, device_id_type=MESH)

    loads = {}

    def load(name, src, dst):
        copy = pltpu.make_async_copy(src, dst, load_sem.at[len(loads)])
        copy.start()
        loads[name] = copy

    half = pl.multiple_of(c * CORE, CORE)
    tokens = pl.ds(pl.multiple_of(c * TOK, TOK), TOK)
    others = pl.ds(pl.multiple_of((1 - c) * TOK, TOK), TOK)
    for j in (0, 1):
        load(("up", j), up_hbm.at[:, pl.ds(half + j * UNIT, UNIT)], ubuf.at[j, y, zl])
    load("quant", quant_hbm.at[:, pl.ds(half, CORE)], quant)
    load("scales", scales_hbm, scales)
    load("latent", latent_hbm, latent)
    load("down", down_hbm, down)
    for s in range(SHARDS):
        load(
            ("cot", s), cot_hbm.at[:, pl.ds(s * SHARD + half, CORE)],
            cot.at[tokens, pl.ds(s * CORE, CORE)],
        )

    def slot(j, da, db):
        dy, dz = (da, db) if j == 0 else (db, da)
        return lax.rem(y + dy + NY, NY), lax.rem(zl + dz + NS, NS)

    def along(j, axis, step):
        return at_y(step) if (j == 0) == (axis == 0) else at_z(step)

    def up_ref(j, da, db, part=None):
        ys, zs = slot(j, da, db)
        ref = ubuf.at[j, ys, zs]
        return ref if part is None else ref.at[part * (RANK // 2):(part + 1) * (RANK // 2)]

    def w_ref(j, da, db, part="fetch"):
        ys, zs = slot(j, da, db)
        ref = wbuf.at[j, ys, zs]
        low = par * EXCL
        if part == "fetch":
            return ref.at[pl.ds(low, FETCH)]
        if part == "h0":
            return ref.at[pl.ds(low, HALF0)]
        if part == "h1":
            return ref.at[pl.ds(low + HALF0, FETCH - HALF0)]
        if part == "top":
            return ref.at[pl.ds(0, LAT // 2)]
        if part == "bottom":
            return ref.at[pl.ds(LAT // 2, LAT // 2)]
        if part == "mine":
            return ref.at[pl.ds(par * FETCH, EXCL)]
        return ref.at[pl.ds((1 - par) * FETCH, EXCL)]

    def up_second(j, da):
        ref = up_ref(j, da, 0)
        send(("u", j, da, -1), ref, ref, along(j, 1, 1))
        send(("u", j, da, 1), ref, ref, along(j, 1, -1))

    def up_start():
        for j in (0, 1):
            ref = up_ref(j, 0, 0)
            send(("u", j, -1, 0), ref, ref, along(j, 0, 1))
            send(("u", j, 1, 0), ref, ref, along(j, 0, -1))
        for j in (0, 1):
            up_second(j, 0)

    def up_pass(j, axis, o, da, name):
        part = 0 if o == -1 else 1
        db = 0 if axis == 0 else o
        ref = up_ref(j, da, db, part)
        send(name + (part,), ref, ref, along(j, axis, -o))

    def up_first(o):
        for j in (0, 1):
            arrived(("u", j, o, 0), up_ref(j, o, 0))
            up_pass(j, 0, o, o, ("u", j, 2, 0))
            up_second(j, o)

    def up_far():
        for j in (0, 1):
            for part in (0, 1):
                arrived(("u", j, 2, 0, part), up_ref(j, 2, 0, part))
            up_second(j, 2)

    def up_turn(da):
        for o in (-1, 1):
            for j in (0, 1):
                arrived(("u", j, da, o), up_ref(j, da, o))
                up_pass(j, 1, o, da, ("u", j, da, 2))

    def up_all():
        for da in (0, -1, 1, 2):
            for j in (0, 1):
                for part in (0, 1):
                    arrived(("u", j, da, 2, part), up_ref(j, da, 2, part))

    def w_second(j, da):
        ref = w_ref(j, da, 0)
        send(("w", j, da, -1), ref, ref, along(j, 1, 1))
        send(("w", j, da, 1), ref, ref, along(j, 1, -1))

    def w_start(j):
        for i in range(LAT // BLOCK):
            for k in range(UNIT // BLOCK):
                col = j * UNIT + k * BLOCK
                block = quant[i * BLOCK:(i + 1) * BLOCK, col:col + BLOCK].astype(jnp.float32)
                wbuf[j, y, zl, i * BLOCK:(i + 1) * BLOCK, k * BLOCK:(k + 1) * BLOCK] = (
                    block * scales[i, c * (CORE // BLOCK) + col // BLOCK]
                ).astype(jnp.bfloat16)
        ref = w_ref(j, 0, 0)
        send(("w", j, -1, 0), ref, ref, along(j, 0, 1))
        send(("w", j, 1, 0), ref, ref, along(j, 0, -1))

    def w_take(j, da, db):
        if (da, db) == (2, 0):
            arrived(("w", j, da, db, 0), w_ref(j, da, db, "h0"))
            arrived(("w", j, da, db, 1), w_ref(j, da, db, "h1"))
        elif db == 2:
            arrived(("w", j, da, db, 0), w_ref(j, da, db, "top"))
            arrived(("w", j, da, db, 1), w_ref(j, da, db, "bottom"))
        else:
            arrived(("w", j, da, db), w_ref(j, da, db))
        if db == 0 and da != 2:
            ref = w_ref(j, da, db, "h0" if da == -1 else "h1")
            send(("w", j, 2, 0, 0 if da == -1 else 1), ref, ref, along(j, 0, -da))

    def w_pass(j, da, db):
        arrived(("wx", j, da, db), w_ref(j, da, db, "missing"))
        ref = w_ref(j, da, db, "top" if db == -1 else "bottom")
        send(("w", j, da, 2, 0 if db == -1 else 1), ref, ref, along(j, 1, -db))

    def w_cross(j, da, db):
        ref = w_ref(j, da, db, "mine")
        send(("wx", j, da, db), ref, ref, at_x(1 if j == 0 else -1))

    def w_ready(da, db):
        for j in (0, 1):
            if db == 0:
                arrived(("wx", j, da, db), w_ref(j, da, db, "missing"))

    def w_use(da, db, rows=slice(None)):
        total = None
        for j in (0, 1):
            ys, zs = slot(j, da, db)
            base = pl.multiple_of((ys * NS + zs) * CORE + j * UNIT, UNIT)
            term = dot_cols(cot[rows, pl.ds(base, UNIT)], wbuf[j, ys, zs])
            total = term if total is None else total + term
        if (da, db) == (0, 0):
            acc[...] = total
        else:
            acc[rows] += total

    def low_start():
        loads["latent"].wait()
        loads["down"].wait()
        low = jnp.dot(
            latent[...], down[...].astype(jnp.float32).T.astype(jnp.bfloat16),
            preferred_element_type=jnp.float32,
        )
        low_t[c] = low.astype(jnp.bfloat16).astype(jnp.float32).T.astype(jnp.bfloat16)
        send("low", low_t.at[c], low_t.at[c], sibling)

    def cot_send():
        for s in range(SHARDS):
            send(
                ("cot", s), cot_hbm.at[:, pl.ds(s * SHARD + CORE - half, CORE)],
                cot.at[tokens, pl.ds(s * CORE, CORE)], sibling,
            )

    def cot_wait(s):
        loads["cot", s].wait()
        arrived(("cot", s), cot.at[others, pl.ds(s * CORE, CORE)])

    def b_terms(g):
        if g == 0:
            arrived("low", low_t.at[1 - c])
        for s in range(g * NS, (g + 1) * NS):
            cot_wait(s)
            cols = slice(s * CORE, (s + 1) * CORE)
            term = jnp.dot(low_t[0], cot[:TOK, cols], preferred_element_type=jnp.float32)
            term += jnp.dot(low_t[1], cot[TOK:, cols], preferred_element_type=jnp.float32)
            own[s] = term
            for k in range(NX):
                x_out[k, s] = term[k * PIECE:(k + 1) * PIECE].astype(jnp.bfloat16)
        part = pl.ds(g * NS, NS)
        for k in (1, 3, 2):
            send(
                ("b1", k, g), x_out.at[lax.rem(x + k, NX), part], x_in.at[k - 1, part], at_x(k)
            )

    def b_x_sum():
        mine = pl.ds(pl.multiple_of(x * PIECE, PIECE), PIECE)
        for g in range(NY):
            for k in (1, 3, 2):
                arrived(("b1", k, g), x_in.at[k - 1, pl.ds(g * NS, NS)])
            for zz in range(NS):
                s = g * NS + zz
                total = own[s, mine]
                for k in range(NX - 1):
                    total = total + x_in[k, s].astype(jnp.float32)
                y_own[g, zz] = total
                y_out[g, zz] = total.astype(jnp.bfloat16)
        for k in (1, 3, 2):
            send(("b2", k), y_out.at[lax.rem(y + k, NY)], y_in.at[k - 1], at_y(k))

    def b_y_sum():
        for k in (1, 3, 2):
            arrived(("b2", k), y_in.at[k - 1])
        for zz in range(NS):
            total = y_own[y, zz]
            for k in range(NY - 1):
                total = total + y_in[k, zz].astype(jnp.float32)
            z_own[zz] = total.astype(jnp.bfloat16)
        z_in[z] = z_own[zl]
        for k in range(1, NZ):
            send(("b3", k), z_own.at[lax.rem(zl + k, NS)], z_in.at[z], at_z(k))

    def b_z_sum():
        for k in range(1, NZ):
            arrived(("b3", k), z_in.at[lax.rem(z + NZ - k, NZ)])
        total = z_in[0].astype(jnp.float32)
        for k in range(1, NZ):
            total = total + z_in[k].astype(jnp.float32)
        gath[me8] = total * FACTOR
        for k in range(1, 8):
            send(("b4", k), gath.at[me8], gath.at[me8], at_8(k))

    def b_write():
        for k in range(1, 8):
            arrived(("b4", k), gath.at[lax.rem(me8 + 8 - k, 8)])
        for p in range(8):
            rows, cols = (p // 2) * PIECE, (p % 2) * CORE
            out_b[rows:rows + PIECE, cols:cols + CORE] = gath[p]

    def a_through():
        def step(s, total):
            for j in (0, 1):
                base = pl.multiple_of(s * CORE + j * UNIT, UNIT)
                total = total + dot_cols(
                    ubuf[j, lax.div(s, NS), lax.rem(s, NS)], cot[:, pl.ds(base, UNIT)]
                )
            return total

        through = lax.fori_loop(0, SHARDS, step, jnp.zeros((RANK, CHIP), jnp.float32), unroll=4)
        for core in (0, 1):
            thr[core] = through[:, core * TOK:(core + 1) * TOK]
        send("thr", thr.at[1 - c], thr_in, sibling)

    def a_terms():
        arrived("thr", thr_in)
        total = (thr[c] + thr_in[...]).astype(jnp.bfloat16)
        thr[c] = total.astype(jnp.float32)
        term = jnp.dot(total, latent[...], preferred_element_type=jnp.float32)
        for p in range(8):
            rows, cols = (p // 2) * PIECE, (p % 2) * (LAT // 2)
            a_own[p] = term[rows:rows + PIECE, cols:cols + LAT // 2]
        for k in range(1, 8):
            send(("a1", k), a_own.at[lax.rem(me8 + k, 8)], a_in.at[k - 1], at_8(k))

    def a_8_sum():
        for k in range(1, 8):
            arrived(("a1", k), a_in.at[k - 1])
        total = a_own[me8]
        for k in range(7):
            total = total + a_in[k]
        ay_in[y] = total
        for k in (1, 3, 2):
            send(("a2", k), ay_in.at[y], ay_in.at[y], at_y(k))

    def a_y_sum():
        for k in (1, 3, 2):
            arrived(("a2", k), ay_in.at[lax.rem(y + NY - k, NY)])
        total = ay_in[0]
        for k in range(1, NY):
            total = total + ay_in[k]
        az_in[z] = total.astype(jnp.bfloat16)
        for k in range(1, NZ):
            send(("a3", k), az_in.at[z], az_in.at[z], at_z(k))

    def a_z_sum():
        for k in range(1, NZ):
            arrived(("a3", k), az_in.at[lax.rem(z + NZ - k, NZ)])
        total = az_in[0].astype(jnp.float32)
        for k in range(1, NZ):
            total = total + az_in[k].astype(jnp.float32)
        a_all[me8] = total * FACTOR
        for k in range(1, 8):
            send(("a4", k), a_all.at[me8], a_all.at[me8], at_8(k))

    def a_write():
        for k in range(1, 8):
            arrived(("a4", k), a_all.at[lax.rem(me8 + 8 - k, 8)])
        for p in range(8):
            rows, cols = (p // 2) * PIECE, (p % 2) * (LAT // 2)
            out_a[rows:rows + PIECE, cols:cols + LAT // 2] = a_all[p]

    def up_wait():
        for j in (0, 1):
            loads["up", j].wait()
        pl.semaphore_wait(barrier, len(partners))

    def take(da, db):
        for j in (0, 1):
            w_take(j, da, db)

    def cross(da, db):
        for j in (0, 1):
            w_cross(j, da, db)

    def second(da):
        for j in (0, 1):
            w_second(j, da)

    def onward(da, db):
        for j in (0, 1):
            w_pass(j, da, db)

    def use(da, db):
        if (da, db) != (0, 0):
            w_ready(da, db)
        w_use(da, db)

    def w_first():
        loads["quant"].wait()
        loads["scales"].wait()
        for j in (0, 1):
            w_start(j)

    up_wait()
    low_start()
    up_start()
    cot_send()
    w_first()
    up_first(-1)
    second(0)
    up_first(1)
    b_terms(0)
    take(-1, 0)
    cross(-1, 0)
    b_terms(1)
    take(1, 0)
    b_terms(2)
    take(0, 1)
    take(0, -1)
    second(1)
    up_far()
    up_turn(1)
    up_turn(-1)
    b_terms(3)
    take(2, 0)
    second(-1)
    up_turn(0)
    take(1, -1)
    cross(0, 1)
    up_turn(2)
    take(1, 1)
    use(0, 0)
    cross(0, -1)
    b_x_sum()
    cross(1, -1)
    cross(1, 1)
    second(2)
    use(-1, 0)
    onward(0, -1)
    cross(1, 0)
    onward(0, 1)
    take(-1, 1)
    use(0, -1)
    cross(2, 0)
    up_all()
    a_through()
    cross(-1, 1)
    take(-1, -1)
    b_y_sum()
    onward(1, -1)
    a_terms()
    take(2, 1)
    cross(-1, -1)
    take(2, -1)
    cross(2, -1)
    use(0, 1)
    cross(2, 1)
    onward(1, 1)
    take(0, 2)
    use(2, 0)
    use(1, 0)
    a_8_sum()
    onward(-1, 1)
    b_z_sum()
    onward(-1, -1)
    use(-1, -1)
    use(-1, 1)
    take(1, 2)
    a_y_sum()
    onward(2, -1)
    onward(2, 1)
    use(2, -1)
    use(1, 1)
    use(2, 1)
    use(0, 2)
    use(1, 2)
    take(-1, 2)
    use(1, -1)
    use(-1, 2)
    a_z_sum()
    take(2, 2)
    b_write()
    w_use(2, 2, others)
    acc_out[...] = acc[others].astype(jnp.bfloat16)
    send("acc", acc_out, acc_in, sibling)
    w_use(2, 2, tokens)
    acc[tokens] += jnp.dot(
        thr[c].T.astype(jnp.bfloat16), down[...], preferred_element_type=jnp.float32
    )
    a_write()
    arrived("acc", acc_in)
    out_lat[...] = (acc[tokens] + acc_in[...].astype(jnp.float32)).astype(jnp.bfloat16)
    for copy in sent:
        copy.wait_send()


def tidy(lat, grad_a, grad_b, out_lat, out_a, out_b):
    out_lat[...] = lat[...]
    out_a[...] = grad_a[...]
    out_b[...] = grad_b[...]


def shards(latent, cotangent, quant, scales, adapter_down, adapter_up):
    vmem = pl.BlockSpec(memory_space=pltpu.VMEM)
    hbm = pl.BlockSpec(memory_space=pl.ANY)
    bf16, f32 = jnp.bfloat16, jnp.float32
    results = (
        jax.ShapeDtypeStruct((TOK, LAT), bf16),
        jax.ShapeDtypeStruct((RANK, LAT), f32),
        jax.ShapeDtypeStruct((RANK, SHARD), f32),
    )
    outs = pl.pallas_call(
        kernel,
        name="adapter_backward",
        out_shape=results,
        in_specs=[hbm] * 6,
        out_specs=(vmem, vmem, vmem),
        scratch_shapes=[
            pltpu.VMEM((TOK, LAT), bf16),
            pltpu.VMEM((RANK, LAT), bf16),
            pltpu.VMEM((LAT, CORE), bf16),
            pltpu.VMEM((CHIP, MINE), bf16),
            pltpu.VMEM((2, NY, NS, LAT, UNIT), bf16),
            pltpu.VMEM((2, NY, NS, RANK, UNIT), bf16),
            pltpu.VMEM((2, RANK, TOK), bf16),
            pltpu.VMEM((CHIP, LAT), f32),
            pltpu.VMEM((TOK, LAT), bf16),
            pltpu.VMEM((TOK, LAT), bf16),
            pltpu.VMEM((2, RANK, TOK), f32),
            pltpu.VMEM((RANK, TOK), f32),
            pltpu.VMEM((SHARDS, RANK, CORE), f32),
            pltpu.VMEM((NX, SHARDS, PIECE, CORE), bf16),
            pltpu.VMEM((NX - 1, SHARDS, PIECE, CORE), bf16),
            pltpu.VMEM((NY, NS, PIECE, CORE), f32),
            pltpu.VMEM((NY, NS, PIECE, CORE), bf16),
            pltpu.VMEM((NY - 1, NS, PIECE, CORE), bf16),
            pltpu.VMEM((NS, PIECE, CORE), bf16),
            pltpu.VMEM((NZ, PIECE, CORE), bf16),
            pltpu.VMEM((8, PIECE, CORE), f32),
            pltpu.VMEM((8, PIECE, LAT // 2), f32),
            pltpu.VMEM((7, PIECE, LAT // 2), f32),
            pltpu.VMEM((NY, PIECE, LAT // 2), f32),
            pltpu.VMEM((NZ, PIECE, LAT // 2), bf16),
            pltpu.VMEM((8, PIECE, LAT // 2), f32),
            pltpu.SMEM((LAT // BLOCK, SHARD // BLOCK), f32),
            pltpu.SemaphoreType.DMA((6 + SHARDS,)),
            pltpu.SemaphoreType.DMA((SENDS,)),
            pltpu.SemaphoreType.DMA((RECVS,)),
        ],
        compiler_params=pltpu.CompilerParams(
            collective_id=0, has_side_effects=True, vmem_limit_bytes=56 * 2**20
        ),
        cost_estimate=pl.CostEstimate(
            flops=2 * TOK * COLS * (LAT + 2 * RANK), bytes_accessed=12 * 2**20, transcendentals=0
        ),
    )(scales, latent, cotangent, quant, adapter_down.T, adapter_up)
    lat, grad_a_t, grad_b = pl.pallas_call(
        tidy,
        name="tidy",
        out_shape=results,
        in_specs=[vmem] * 3,
        out_specs=(vmem, vmem, vmem),
    )(*outs)
    return lat, grad_a_t.T, grad_b


def solution(mesh):
    placed = (
        P(("dp", "fsdp"), None),
        P(("dp", "fsdp"), None),
        P(None, "fsdp"),
        P(None, "fsdp"),
        P(),
        P(None, "fsdp"),
    )
    return jax.shard_map(
        shards,
        mesh=mesh,
        in_specs=placed,
        out_specs=(P(("dp", "fsdp"), None), P(), P(None, "fsdp")),
        check_vma=False,
    )
```

```python
import jax
import jax.numpy as jnp
from jax import lax
from jax.experimental import pallas as pl
from jax.experimental.pallas import tpu as pltpu
from jax.sharding import PartitionSpec as P

MESH = pl.DeviceIdType.MESH
BLOCK = 128
NX, NY, NZ = 4, 4, 8
NS = 4
TOK, COLS, LAT, RANK = 256, 16384, 512, 64
SHARD = COLS // (NY * NS)
CORE = SHARD // 2
UNIT = CORE // 2
SHARDS = NY * NS
MINE = COLS // 2
CHIP = 2 * TOK
PIECE = RANK // NX
EXCL = 160
FETCH = LAT - EXCL
HALF0 = FETCH // 32 * 16
FACTOR = 1.0 / 65536.0 ** 0.5
SENDS = 208
RECVS = 208

ORDER = [
    (-1, 0), (1, 0), (0, -1), (0, 1), (2, 0),
    (-1, -1), (-1, 1), (1, -1), (1, 1),
    (0, 2), (2, -1), (2, 1), (-1, 2), (1, 2), (2, 2),
]


def dot_cols(left, right):
    return lax.dot_general(
        left, right, (((1,), (1,)), ((), ())), preferred_element_type=jnp.float32
    )


def kernel(
    scales_hbm, latent_hbm, cot_hbm, quant_hbm, down_hbm, up_hbm,
    out_lat, out_a, out_b,
    latent, down, quant, cot, wbuf, ubuf, low_t, acc, acc_out, acc_in, thr, thr_in, own, x_out, x_in,
    y_own, y_out, y_in, z_own, z_in, gath,
    a_own, a_in, ay_in, az_in, a_all,
    lat_done, a_done, b_done, scales, load_sem, send_sem, recv_sem,
):
    d, f = lax.axis_index("dp"), lax.axis_index("fsdp")
    x, c = lax.div(d, 4), lax.rem(d, 2)
    y, zl = lax.div(f, 4), lax.rem(f, 4)
    z = lax.rem(lax.div(d, 2), 2) * 4 + zl
    par = lax.rem(x, 2)
    me8 = x * 2 + c

    def dev(xx, yy, zz, cc):
        return (xx * 4 + lax.div(zz, 4) * 2 + cc, yy * 4 + lax.rem(zz, 4))

    def at_x(k):
        return dev(lax.rem(x + k + NX, NX), y, z, c)

    def at_y(k):
        return dev(x, lax.rem(y + k + NY, NY), z, c)

    def at_z(k):
        return dev(x, y, lax.rem(z + k + NZ, NZ), c)

    def at_8(k):
        p = lax.rem(me8 + k, 8)
        return dev(lax.div(p, 2), y, z, lax.rem(p, 2))

    sibling = dev(x, y, z, 1 - c)

    sent = []
    events = {}

    def event(name):
        return recv_sem.at[events.setdefault(name, len(events))]

    def send(name, src, dst, target):
        copy = pltpu.make_async_remote_copy(
            src_ref=src, dst_ref=dst, send_sem=send_sem.at[len(sent)],
            recv_sem=event(name), device_id=target, device_id_type=MESH,
        )
        copy.start()
        sent.append(copy)

    def arrived(name, dst):
        pltpu.make_async_remote_copy(
            src_ref=dst, dst_ref=dst, send_sem=send_sem.at[0],
            recv_sem=event(name), device_id=sibling, device_id_type=MESH,
        ).wait_recv()

    barrier = pltpu.get_barrier_semaphore()
    partners = (
        [at_8(k) for k in range(1, 8)]
        + [at_y(k) for k in range(1, NY)]
        + [at_z(k) for k in range(1, NZ)]
    )
    for partner in partners:
        pl.semaphore_signal(barrier, inc=1, device_id=partner, device_id_type=MESH)

    loads = {}

    def load(name, src, dst):
        copy = pltpu.make_async_copy(src, dst, load_sem.at[len(loads)])
        copy.start()
        loads[name] = copy

    stores = []

    def store(src, dst):
        copy = pltpu.make_async_copy(src, dst, load_sem.at[6 + SHARDS + len(stores)])
        copy.start()
        stores.append(copy)

    half = pl.multiple_of(c * CORE, CORE)
    tokens = pl.ds(pl.multiple_of(c * TOK, TOK), TOK)
    others = pl.ds(pl.multiple_of((1 - c) * TOK, TOK), TOK)
    for j in (0, 1):
        load(("up", j), up_hbm.at[:, pl.ds(half + j * UNIT, UNIT)], ubuf.at[j, y, zl])
    load("quant", quant_hbm.at[:, pl.ds(half, CORE)], quant)
    load("scales", scales_hbm, scales)
    load("latent", latent_hbm, latent.at[tokens])
    load("down", down_hbm, down)
    for s in range(SHARDS):
        load(
            ("cot", s), cot_hbm.at[:, pl.ds(s * SHARD + half, CORE)],
            cot.at[tokens, pl.ds(s * CORE, CORE)],
        )

    def slot(j, da, db):
        dy, dz = (da, db) if j == 0 else (db, da)
        return lax.rem(y + dy + NY, NY), lax.rem(zl + dz + NS, NS)

    def along(j, axis, step):
        return at_y(step) if (j == 0) == (axis == 0) else at_z(step)

    def up_ref(j, da, db, part=None):
        ys, zs = slot(j, da, db)
        ref = ubuf.at[j, ys, zs]
        return ref if part is None else ref.at[part * (RANK // 2):(part + 1) * (RANK // 2)]

    def w_ref(j, da, db, part="fetch"):
        ys, zs = slot(j, da, db)
        ref = wbuf.at[j, ys, zs]
        low = par * EXCL
        if part == "fetch":
            return ref.at[pl.ds(low, FETCH)]
        if part == "h0":
            return ref.at[pl.ds(low, HALF0)]
        if part == "h1":
            return ref.at[pl.ds(low + HALF0, FETCH - HALF0)]
        if part == "top":
            return ref.at[pl.ds(0, LAT // 2)]
        if part == "bottom":
            return ref.at[pl.ds(LAT // 2, LAT // 2)]
        if part == "mine":
            return ref.at[pl.ds(par * FETCH, EXCL)]
        return ref.at[pl.ds((1 - par) * FETCH, EXCL)]

    def up_second(j, da):
        ref = up_ref(j, da, 0)
        send(("u", j, da, -1), ref, ref, along(j, 1, 1))
        send(("u", j, da, 1), ref, ref, along(j, 1, -1))

    def up_start():
        for j in (0, 1):
            ref = up_ref(j, 0, 0)
            send(("u", j, -1, 0), ref, ref, along(j, 0, 1))
            send(("u", j, 1, 0), ref, ref, along(j, 0, -1))
        for j in (0, 1):
            up_second(j, 0)

    def up_pass(j, axis, o, da, name):
        part = 0 if o == -1 else 1
        db = 0 if axis == 0 else o
        ref = up_ref(j, da, db, part)
        send(name + (part,), ref, ref, along(j, axis, -o))

    def up_first(o):
        for j in (0, 1):
            arrived(("u", j, o, 0), up_ref(j, o, 0))
            up_pass(j, 0, o, o, ("u", j, 2, 0))
            up_second(j, o)

    def up_far():
        for j in (0, 1):
            for part in (0, 1):
                arrived(("u", j, 2, 0, part), up_ref(j, 2, 0, part))
            up_second(j, 2)

    def up_turn(da):
        for o in (-1, 1):
            for j in (0, 1):
                arrived(("u", j, da, o), up_ref(j, da, o))
                up_pass(j, 1, o, da, ("u", j, da, 2))

    def up_all():
        for da in (-1, 1, 2, 0):
            for j in (0, 1):
                for part in (0, 1):
                    arrived(("u", j, da, 2, part), up_ref(j, da, 2, part))

    def w_second(j, da):
        ref = w_ref(j, da, 0)
        send(("w", j, da, -1), ref, ref, along(j, 1, 1))
        send(("w", j, da, 1), ref, ref, along(j, 1, -1))

    def w_start(j):
        for i in range(LAT // BLOCK):
            for k in range(UNIT // BLOCK):
                col = j * UNIT + k * BLOCK
                block = quant[i * BLOCK:(i + 1) * BLOCK, col:col + BLOCK].astype(jnp.float32)
                wbuf[j, y, zl, i * BLOCK:(i + 1) * BLOCK, k * BLOCK:(k + 1) * BLOCK] = (
                    block * scales[i, c * (CORE // BLOCK) + col // BLOCK]
                ).astype(jnp.bfloat16)
        ref = w_ref(j, 0, 0)
        send(("w", j, -1, 0), ref, ref, along(j, 0, 1))
        send(("w", j, 1, 0), ref, ref, along(j, 0, -1))

    def w_take(j, da, db):
        if (da, db) == (2, 0):
            arrived(("w", j, da, db, 0), w_ref(j, da, db, "h0"))
            arrived(("w", j, da, db, 1), w_ref(j, da, db, "h1"))
        elif db == 2:
            arrived(("w", j, da, db, 0), w_ref(j, da, db, "top"))
            arrived(("w", j, da, db, 1), w_ref(j, da, db, "bottom"))
        else:
            arrived(("w", j, da, db), w_ref(j, da, db))
        if db == 0 and da != 2:
            ref = w_ref(j, da, db, "h0" if da == -1 else "h1")
            send(("w", j, 2, 0, 0 if da == -1 else 1), ref, ref, along(j, 0, -da))

    def w_pass(j, da, db):
        arrived(("wx", j, da, db), w_ref(j, da, db, "missing"))
        ref = w_ref(j, da, db, "top" if db == -1 else "bottom")
        send(("w", j, da, 2, 0 if db == -1 else 1), ref, ref, along(j, 1, -db))

    def w_cross(j, da, db):
        ref = w_ref(j, da, db, "mine")
        send(("wx", j, da, db), ref, ref, at_x(1 if j == 0 else -1))

    def w_ready(da, db):
        for j in (0, 1):
            if db == 0:
                arrived(("wx", j, da, db), w_ref(j, da, db, "missing"))

    def w_use(da, db, rows=slice(None)):
        total = None
        for j in (0, 1):
            ys, zs = slot(j, da, db)
            base = pl.multiple_of((ys * NS + zs) * CORE + j * UNIT, UNIT)
            term = dot_cols(cot[rows, pl.ds(base, UNIT)], wbuf[j, ys, zs])
            total = term if total is None else total + term
        if (da, db) == (0, 0):
            acc[...] = total
        else:
            acc[rows] += total

    def low_start():
        loads["latent"].wait()
        loads["down"].wait()
        low = jnp.dot(
            latent[tokens], down[...].astype(jnp.float32).T.astype(jnp.bfloat16),
            preferred_element_type=jnp.float32,
        )
        low_t[c] = low.astype(jnp.bfloat16).astype(jnp.float32).T.astype(jnp.bfloat16)
        send("low", low_t.at[c], low_t.at[c], sibling)
        send("latent", latent.at[tokens], latent.at[tokens], sibling)

    def cot_send():
        for s in range(SHARDS):
            send(
                ("cot", s), cot_hbm.at[:, pl.ds(s * SHARD + CORE - half, CORE)],
                cot.at[tokens, pl.ds(s * CORE, CORE)], sibling,
            )

    def cot_wait(s):
        loads["cot", s].wait()
        arrived(("cot", s), cot.at[others, pl.ds(s * CORE, CORE)])

    def b_terms(g):
        if g == 0:
            arrived("low", low_t.at[1 - c])
        for s in range(g * NS, (g + 1) * NS):
            cot_wait(s)
            cols = slice(s * CORE, (s + 1) * CORE)
            term = jnp.dot(low_t[0], cot[:TOK, cols], preferred_element_type=jnp.float32)
            term += jnp.dot(low_t[1], cot[TOK:, cols], preferred_element_type=jnp.float32)
            own[s] = term
            for k in range(NX):
                x_out[k, s] = term[k * PIECE:(k + 1) * PIECE].astype(jnp.bfloat16)
        part = pl.ds(g * NS, NS)
        for k in (1, 3, 2):
            send(
                ("b1", k, g), x_out.at[lax.rem(x + k, NX), part], x_in.at[k - 1, part], at_x(k)
            )

    def b_x_sum():
        mine = pl.ds(pl.multiple_of(x * PIECE, PIECE), PIECE)
        for g in range(NY):
            for k in (1, 3, 2):
                arrived(("b1", k, g), x_in.at[k - 1, pl.ds(g * NS, NS)])
            for zz in range(NS):
                s = g * NS + zz
                total = own[s, mine]
                for k in range(NX - 1):
                    total = total + x_in[k, s].astype(jnp.float32)
                y_own[g, zz] = total
                y_out[g, zz] = total.astype(jnp.bfloat16)
        for k in (1, 3, 2):
            send(("b2", k), y_out.at[lax.rem(y + k, NY)], y_in.at[k - 1], at_y(k))

    def b_y_sum():
        for k in (1, 3, 2):
            arrived(("b2", k), y_in.at[k - 1])
        for zz in range(NS):
            total = y_own[y, zz]
            for k in range(NY - 1):
                total = total + y_in[k, zz].astype(jnp.float32)
            z_own[zz] = total.astype(jnp.bfloat16)
        z_in[z] = z_own[zl]
        for k in range(1, NZ):
            send(("b3", k), z_own.at[lax.rem(zl + k, NS)], z_in.at[z], at_z(k))

    def b_z_sum():
        for k in range(1, NZ):
            arrived(("b3", k), z_in.at[lax.rem(z + NZ - k, NZ)])
        total = z_in[0].astype(jnp.float32)
        for k in range(1, NZ):
            total = total + z_in[k].astype(jnp.float32)
        gath[me8] = total * FACTOR
        for k in range(1, 8):
            send(("b4", k), gath.at[me8], gath.at[me8], at_8(k))

    def b_write():
        for k in range(1, 8):
            arrived(("b4", k), gath.at[lax.rem(me8 + 8 - k, 8)])
        for p in range(8):
            rows, cols = (p // 2) * PIECE, (p % 2) * CORE
            b_done[rows:rows + PIECE, cols:cols + CORE] = gath[p]
        store(b_done, out_b)

    def a_through(*dbs):
        total = None
        for db in dbs:
            for da in (0, -1, 1, 2):
                for j in (0, 1):
                    ys, zs = slot(j, da, db)
                    base = pl.multiple_of((ys * NS + zs) * CORE + j * UNIT, UNIT)
                    term = dot_cols(ubuf[j, ys, zs], cot[:, pl.ds(base, UNIT)])
                    total = term if total is None else total + term
        for core in (0, 1):
            part = total[:, core * TOK:(core + 1) * TOK]
            if 0 in dbs:
                thr[core] = part
            else:
                thr[core] += part

    def a_terms():
        arrived("latent", latent.at[others])
        send("thr", thr.at[1 - c], thr_in, sibling)
        term = jnp.dot(
            thr[0].astype(jnp.bfloat16), latent[:TOK], preferred_element_type=jnp.float32
        )
        term += jnp.dot(
            thr[1].astype(jnp.bfloat16), latent[TOK:], preferred_element_type=jnp.float32
        )
        for p in range(8):
            rows, cols = (p // 2) * PIECE, (p % 2) * (LAT // 2)
            a_own[p] = term[rows:rows + PIECE, cols:cols + LAT // 2]
        for k in range(1, 8):
            send(("a1", k), a_own.at[lax.rem(me8 + k, 8)], a_in.at[k - 1], at_8(k))

    def a_8_sum():
        for k in range(1, 8):
            arrived(("a1", k), a_in.at[k - 1])
        total = a_own[me8]
        for k in range(7):
            total = total + a_in[k]
        ay_in[y] = total
        for k in (1, 3, 2):
            send(("a2", k), ay_in.at[y], ay_in.at[y], at_y(k))

    def a_y_sum():
        for k in (1, 3, 2):
            arrived(("a2", k), ay_in.at[lax.rem(y + NY - k, NY)])
        total = ay_in[0]
        for k in range(1, NY):
            total = total + ay_in[k]
        az_in[z] = total.astype(jnp.bfloat16)
        for k in range(1, NZ):
            send(("a3", k), az_in.at[z], az_in.at[z], at_z(k))

    def a_z_sum():
        for k in range(1, NZ):
            arrived(("a3", k), az_in.at[lax.rem(z + NZ - k, NZ)])
        total = az_in[0].astype(jnp.float32)
        for k in range(1, NZ):
            total = total + az_in[k].astype(jnp.float32)
        a_all[me8] = total * FACTOR
        for k in range(1, 8):
            send(("a4", k), a_all.at[me8], a_all.at[me8], at_8(k))

    def a_write():
        for k in range(1, 8):
            arrived(("a4", k), a_all.at[lax.rem(me8 + 8 - k, 8)])
        for p in range(8):
            rows, cols = (p // 2) * PIECE, (p % 2) * (LAT // 2)
            a_done[rows:rows + PIECE, cols:cols + LAT // 2] = a_all[p]
        store(a_done, out_a)

    def up_wait():
        for j in (0, 1):
            loads["up", j].wait()
        pl.semaphore_wait(barrier, len(partners))

    def take(da, db):
        for j in (0, 1):
            w_take(j, da, db)

    def cross(da, db):
        for j in (0, 1):
            w_cross(j, da, db)

    def second(da):
        for j in (0, 1):
            w_second(j, da)

    def onward(da, db):
        for j in (0, 1):
            w_pass(j, da, db)

    def use(da, db):
        if (da, db) != (0, 0):
            w_ready(da, db)
        w_use(da, db)

    def w_first():
        loads["quant"].wait()
        loads["scales"].wait()
        for j in (0, 1):
            w_start(j)

    up_wait()
    up_start()
    low_start()
    w_first()
    cot_send()
    second(0)
    up_first(-1)
    b_terms(0)
    up_turn(0)
    take(-1, 0)
    up_first(1)
    cross(-1, 0)
    second(-1)
    b_terms(1)
    take(0, -1)
    take(0, 1)
    take(1, 0)
    cross(0, -1)
    up_far()
    b_terms(2)
    up_turn(1)
    second(1)
    up_turn(-1)
    b_terms(3)
    take(-1, 1)
    a_through(0)
    up_turn(2)
    cross(0, 1)
    take(2, 0)
    cross(-1, 1)
    second(2)
    a_through(-1, 1)
    take(1, -1)
    cross(1, -1)
    use(0, 0)
    b_x_sum()
    up_all()
    take(-1, -1)
    onward(0, 1)
    a_through(2)
    take(1, 1)
    onward(0, -1)
    cross(1, 1)
    a_terms()
    onward(-1, 1)
    take(2, 1)
    use(-1, 1)
    cross(1, 0)
    use(0, 1)
    take(2, -1)
    cross(-1, -1)
    cross(2, -1)
    use(0, -1)
    onward(1, -1)
    b_y_sum()
    take(0, 2)
    use(1, -1)
    a_8_sum()
    use(-1, 0)
    use(0, 2)
    cross(2, 1)
    onward(-1, -1)
    onward(1, 1)
    use(-1, -1)
    use(1, 0)
    cross(2, 0)
    use(1, 1)
    a_y_sum()
    b_z_sum()
    onward(2, -1)
    onward(2, 1)
    take(1, 2)
    use(1, 2)
    take(-1, 2)
    use(2, 0)
    use(2, 1)
    use(2, -1)
    use(-1, 2)
    a_z_sum()
    b_write()
    take(2, 2)
    w_use(2, 2, others)
    acc_out[...] = acc[others].astype(jnp.bfloat16)
    send("acc", acc_out, acc_in, sibling)
    w_use(2, 2, tokens)
    arrived("thr", thr_in)
    through = (thr[c] + thr_in[...]).T.astype(jnp.bfloat16)
    acc[tokens] += jnp.dot(through, down[...], preferred_element_type=jnp.float32)
    a_write()
    arrived("acc", acc_in)
    lat_done[...] = (acc[tokens] + acc_in[...].astype(jnp.float32)).astype(jnp.bfloat16)
    store(lat_done, out_lat)
    for copy in sent:
        copy.wait_send()
    for copy in stores:
        copy.wait()


def tidy(lat, grad_a, grad_b, out_lat, out_a, out_b, lat_held, a_held, b_held, in_sem, out_sem):
    moves = ((grad_b, b_held, out_b), (lat, lat_held, out_lat), (grad_a, a_held, out_a))
    reads = [pltpu.make_async_copy(m[0], m[1], in_sem.at[i]) for i, m in enumerate(moves)]
    writes = [pltpu.make_async_copy(m[1], m[2], out_sem.at[i]) for i, m in enumerate(moves)]
    for read in reads:
        read.start()
    for read, write in zip(reads, writes):
        read.wait()
        write.start()
    for write in writes:
        write.wait()


def shards(latent, cotangent, quant, scales, adapter_down, adapter_up):
    hbm = pl.BlockSpec(memory_space=pl.ANY)
    bf16, f32 = jnp.bfloat16, jnp.float32
    results = (
        jax.ShapeDtypeStruct((TOK, LAT), bf16),
        jax.ShapeDtypeStruct((RANK, LAT), f32),
        jax.ShapeDtypeStruct((RANK, SHARD), f32),
    )
    outs = pl.pallas_call(
        kernel,
        name="adapter_backward",
        out_shape=results,
        in_specs=[hbm] * 6,
        out_specs=(hbm, hbm, hbm),
        scratch_shapes=[
            pltpu.VMEM((CHIP, LAT), bf16),
            pltpu.VMEM((RANK, LAT), bf16),
            pltpu.VMEM((LAT, CORE), bf16),
            pltpu.VMEM((CHIP, MINE), bf16),
            pltpu.VMEM((2, NY, NS, LAT, UNIT), bf16),
            pltpu.VMEM((2, NY, NS, RANK, UNIT), bf16),
            pltpu.VMEM((2, RANK, TOK), bf16),
            pltpu.VMEM((CHIP, LAT), f32),
            pltpu.VMEM((TOK, LAT), bf16),
            pltpu.VMEM((TOK, LAT), bf16),
            pltpu.VMEM((2, RANK, TOK), f32),
            pltpu.VMEM((RANK, TOK), f32),
            pltpu.VMEM((SHARDS, RANK, CORE), f32),
            pltpu.VMEM((NX, SHARDS, PIECE, CORE), bf16),
            pltpu.VMEM((NX - 1, SHARDS, PIECE, CORE), bf16),
            pltpu.VMEM((NY, NS, PIECE, CORE), f32),
            pltpu.VMEM((NY, NS, PIECE, CORE), bf16),
            pltpu.VMEM((NY - 1, NS, PIECE, CORE), bf16),
            pltpu.VMEM((NS, PIECE, CORE), bf16),
            pltpu.VMEM((NZ, PIECE, CORE), bf16),
            pltpu.VMEM((8, PIECE, CORE), f32),
            pltpu.VMEM((8, PIECE, LAT // 2), f32),
            pltpu.VMEM((7, PIECE, LAT // 2), f32),
            pltpu.VMEM((NY, PIECE, LAT // 2), f32),
            pltpu.VMEM((NZ, PIECE, LAT // 2), bf16),
            pltpu.VMEM((8, PIECE, LAT // 2), f32),
            pltpu.VMEM((TOK, LAT), bf16),
            pltpu.VMEM((RANK, LAT), f32),
            pltpu.VMEM((RANK, SHARD), f32),
            pltpu.SMEM((LAT // BLOCK, SHARD // BLOCK), f32),
            pltpu.SemaphoreType.DMA((9 + SHARDS,)),
            pltpu.SemaphoreType.DMA((SENDS,)),
            pltpu.SemaphoreType.DMA((RECVS,)),
        ],
        compiler_params=pltpu.CompilerParams(
            collective_id=0, has_side_effects=True, vmem_limit_bytes=56 * 2**20
        ),
        cost_estimate=pl.CostEstimate(
            flops=2 * TOK * COLS * (LAT + 2 * RANK), bytes_accessed=12 * 2**20, transcendentals=0
        ),
    )(scales, latent, cotangent, quant, adapter_down.T, adapter_up)
    lat, grad_a_t, grad_b = pl.pallas_call(
        tidy,
        name="tidy",
        out_shape=results,
        in_specs=[hbm] * 3,
        out_specs=(hbm, hbm, hbm),
        scratch_shapes=[
            pltpu.VMEM((TOK, LAT), bf16),
            pltpu.VMEM((RANK, LAT), f32),
            pltpu.VMEM((RANK, SHARD), f32),
            pltpu.SemaphoreType.DMA((3,)),
            pltpu.SemaphoreType.DMA((3,)),
        ],
    )(*outs)
    return lat, grad_a_t.T, grad_b


def solution(mesh):
    placed = (
        P(("dp", "fsdp"), None),
        P(("dp", "fsdp"), None),
        P(None, "fsdp"),
        P(None, "fsdp"),
        P(),
        P(None, "fsdp"),
    )
    return jax.shard_map(
        shards,
        mesh=mesh,
        in_specs=placed,
        out_specs=(P(("dp", "fsdp"), None), P(), P(None, "fsdp")),
        check_vma=False,
    )
```

```python
import jax
import jax.numpy as jnp
from jax import lax
from jax.experimental import pallas as pl
from jax.experimental.pallas import tpu as pltpu
from jax.sharding import PartitionSpec as P

MESH = pl.DeviceIdType.MESH
BLOCK = 128
NX, NY, NZ = 4, 4, 8
NS = 4
TOK, COLS, LAT, RANK = 256, 16384, 512, 64
SHARD = COLS // (NY * NS)
CORE = SHARD // 2
UNIT = CORE // 2
SHARDS = NY * NS
MINE = COLS // 2
CHIP = 2 * TOK
PIECE = RANK // NX
EXCL = 160
FETCH = LAT - EXCL
HALF0 = FETCH // 32 * 16
FACTOR = 1.0 / 65536.0 ** 0.5
SENDS = 216
RECVS = 216

ORDER = [
    (-1, 0), (1, 0), (0, -1), (0, 1), (2, 0),
    (-1, -1), (-1, 1), (1, -1), (1, 1),
    (0, 2), (2, -1), (2, 1), (-1, 2), (1, 2), (2, 2),
]


def dot_cols(left, right):
    return lax.dot_general(
        left, right, (((1,), (1,)), ((), ())), preferred_element_type=jnp.float32
    )


def kernel(
    scales_hbm, latent_hbm, cot_hbm, quant_hbm, down_hbm, up_hbm,
    out_lat, out_a, out_b,
    latent, down, quant, cot, wbuf, ubuf, low_t, acc, acc_out, acc_in, thr, thr_in, own, x_out, x_in,
    y_own, y_out, y_in, z_own, z_in, gath,
    a_own, a_in, ay_in, az_in, a_all,
    lat_done, a_done, b_done, scales, load_sem, send_sem, recv_sem,
):
    d, f = lax.axis_index("dp"), lax.axis_index("fsdp")
    x, c = lax.div(d, 4), lax.rem(d, 2)
    y, zl = lax.div(f, 4), lax.rem(f, 4)
    z = lax.rem(lax.div(d, 2), 2) * 4 + zl
    par = lax.rem(x, 2)
    me8 = x * 2 + c

    def dev(xx, yy, zz, cc):
        return (xx * 4 + lax.div(zz, 4) * 2 + cc, yy * 4 + lax.rem(zz, 4))

    def at_x(k):
        return dev(lax.rem(x + k + NX, NX), y, z, c)

    def at_y(k):
        return dev(x, lax.rem(y + k + NY, NY), z, c)

    def at_z(k):
        return dev(x, y, lax.rem(z + k + NZ, NZ), c)

    def at_8(k):
        p = lax.rem(me8 + k, 8)
        return dev(lax.div(p, 2), y, z, lax.rem(p, 2))

    sibling = dev(x, y, z, 1 - c)

    sent = []
    events = {}

    def event(name):
        return recv_sem.at[events.setdefault(name, len(events))]

    def send(name, src, dst, target):
        copy = pltpu.make_async_remote_copy(
            src_ref=src, dst_ref=dst, send_sem=send_sem.at[len(sent)],
            recv_sem=event(name), device_id=target, device_id_type=MESH,
        )
        copy.start()
        sent.append(copy)

    def arrived(name, dst):
        pltpu.make_async_remote_copy(
            src_ref=dst, dst_ref=dst, send_sem=send_sem.at[0],
            recv_sem=event(name), device_id=sibling, device_id_type=MESH,
        ).wait_recv()

    barrier = pltpu.get_barrier_semaphore()
    partners = (
        [at_8(k) for k in range(1, 8)]
        + [at_y(k) for k in range(1, NY)]
        + [at_z(k) for k in range(1, NZ)]
    )
    for partner in partners:
        pl.semaphore_signal(barrier, inc=1, device_id=partner, device_id_type=MESH)

    loads = {}

    def load(name, src, dst):
        copy = pltpu.make_async_copy(src, dst, load_sem.at[len(loads)])
        copy.start()
        loads[name] = copy

    stores = []

    def store(src, dst):
        copy = pltpu.make_async_copy(src, dst, load_sem.at[6 + SHARDS + len(stores)])
        copy.start()
        stores.append(copy)

    half = pl.multiple_of(c * CORE, CORE)
    tokens = pl.ds(pl.multiple_of(c * TOK, TOK), TOK)
    others = pl.ds(pl.multiple_of((1 - c) * TOK, TOK), TOK)
    for j in (0, 1):
        load(("up", j), up_hbm.at[:, pl.ds(half + j * UNIT, UNIT)], ubuf.at[j, y, zl])
    load("quant", quant_hbm.at[:, pl.ds(half, CORE)], quant)
    load("scales", scales_hbm, scales)
    load("latent", latent_hbm, latent.at[tokens])
    load("down", down_hbm, down)
    for s in range(SHARDS):
        load(
            ("cot", s), cot_hbm.at[:, pl.ds(s * SHARD + half, CORE)],
            cot.at[tokens, pl.ds(s * CORE, CORE)],
        )

    def slot(j, da, db):
        dy, dz = (da, db) if j == 0 else (db, da)
        return lax.rem(y + dy + NY, NY), lax.rem(zl + dz + NS, NS)

    def along(j, axis, step):
        return at_y(step) if (j == 0) == (axis == 0) else at_z(step)

    def up_ref(j, da, db, part=None):
        ys, zs = slot(j, da, db)
        ref = ubuf.at[j, ys, zs]
        return ref if part is None else ref.at[part * (RANK // 2):(part + 1) * (RANK // 2)]

    def w_ref(j, da, db, part="fetch"):
        ys, zs = slot(j, da, db)
        ref = wbuf.at[j, ys, zs]
        low = par * EXCL
        if part == "fetch":
            return ref.at[pl.ds(low, FETCH)]
        if part == "h0":
            return ref.at[pl.ds(low, HALF0)]
        if part == "h1":
            return ref.at[pl.ds(low + HALF0, FETCH - HALF0)]
        if part == "top":
            return ref.at[pl.ds(0, LAT // 2)]
        if part == "bottom":
            return ref.at[pl.ds(LAT // 2, LAT // 2)]
        if part == "mine":
            return ref.at[pl.ds(par * FETCH, EXCL)]
        return ref.at[pl.ds((1 - par) * FETCH, EXCL)]

    def up_second(j, da):
        ref = up_ref(j, da, 0)
        send(("u", j, da, -1), ref, ref, along(j, 1, 1))
        send(("u", j, da, 1), ref, ref, along(j, 1, -1))

    def up_start():
        for j in (0, 1):
            ref = up_ref(j, 0, 0)
            send(("u", j, -1, 0), ref, ref, along(j, 0, 1))
            send(("u", j, 1, 0), ref, ref, along(j, 0, -1))
        for j in (0, 1):
            up_second(j, 0)

    def up_pass(j, axis, o, da, name):
        part = 0 if o == -1 else 1
        db = 0 if axis == 0 else o
        ref = up_ref(j, da, db, part)
        send(name + (part,), ref, ref, along(j, axis, -o))

    def up_first(o):
        for j in (0, 1):
            arrived(("u", j, o, 0), up_ref(j, o, 0))
            up_pass(j, 0, o, o, ("u", j, 2, 0))
            up_second(j, o)

    def up_far():
        for j in (0, 1):
            for part in (0, 1):
                arrived(("u", j, 2, 0, part), up_ref(j, 2, 0, part))
            up_second(j, 2)

    def up_turn(da):
        for o in (-1, 1):
            for j in (0, 1):
                arrived(("u", j, da, o), up_ref(j, da, o))
                up_pass(j, 1, o, da, ("u", j, da, 2))

    def up_all():
        for da in (-1, 1, 2, 0):
            for j in (0, 1):
                for part in (0, 1):
                    arrived(("u", j, da, 2, part), up_ref(j, da, 2, part))

    def w_second(j, da):
        ref = w_ref(j, da, 0)
        send(("w", j, da, -1), ref, ref, along(j, 1, 1))
        send(("w", j, da, 1), ref, ref, along(j, 1, -1))

    def w_start(j):
        for i in range(LAT // BLOCK):
            for k in range(UNIT // BLOCK):
                col = j * UNIT + k * BLOCK
                block = quant[i * BLOCK:(i + 1) * BLOCK, col:col + BLOCK].astype(jnp.float32)
                wbuf[j, y, zl, i * BLOCK:(i + 1) * BLOCK, k * BLOCK:(k + 1) * BLOCK] = (
                    block * scales[i, c * (CORE // BLOCK) + col // BLOCK]
                ).astype(jnp.bfloat16)
        ref = w_ref(j, 0, 0)
        send(("w", j, -1, 0), ref, ref, along(j, 0, 1))
        send(("w", j, 1, 0), ref, ref, along(j, 0, -1))

    def w_take(j, da, db):
        if (da, db) == (2, 0):
            arrived(("w", j, da, db, 0), w_ref(j, da, db, "h0"))
            arrived(("w", j, da, db, 1), w_ref(j, da, db, "h1"))
        elif db == 2:
            arrived(("w", j, da, db, 0), w_ref(j, da, db, "top"))
            arrived(("w", j, da, db, 1), w_ref(j, da, db, "bottom"))
        else:
            arrived(("w", j, da, db), w_ref(j, da, db))
        if db == 0 and da != 2:
            ref = w_ref(j, da, db, "h0" if da == -1 else "h1")
            send(("w", j, 2, 0, 0 if da == -1 else 1), ref, ref, along(j, 0, -da))

    def w_pass(j, da, db):
        arrived(("wx", j, da, db), w_ref(j, da, db, "missing"))
        ref = w_ref(j, da, db, "top" if db == -1 else "bottom")
        send(("w", j, da, 2, 0 if db == -1 else 1), ref, ref, along(j, 1, -db))

    def w_cross(j, da, db):
        ref = w_ref(j, da, db, "mine")
        send(("wx", j, da, db), ref, ref, at_x(1 if j == 0 else -1))

    def w_ready(da, db):
        for j in (0, 1):
            if db == 0:
                arrived(("wx", j, da, db), w_ref(j, da, db, "missing"))

    def w_use(da, db, rows=slice(None)):
        total = None
        for j in (0, 1):
            ys, zs = slot(j, da, db)
            base = pl.multiple_of((ys * NS + zs) * CORE + j * UNIT, UNIT)
            term = dot_cols(cot[rows, pl.ds(base, UNIT)], wbuf[j, ys, zs])
            total = term if total is None else total + term
        if (da, db) == (0, 0):
            acc[...] = total
        else:
            acc[rows] += total

    def low_start():
        loads["latent"].wait()
        loads["down"].wait()
        low = jnp.dot(
            latent[tokens], down[...].astype(jnp.float32).T.astype(jnp.bfloat16),
            preferred_element_type=jnp.float32,
        )
        low_t[c] = low.astype(jnp.bfloat16).astype(jnp.float32).T.astype(jnp.bfloat16)
        send("low", low_t.at[c], low_t.at[c], sibling)
        send("latent", latent.at[tokens], latent.at[tokens], sibling)

    def cot_send():
        for s in range(SHARDS):
            send(
                ("cot", s), cot_hbm.at[:, pl.ds(s * SHARD + CORE - half, CORE)],
                cot.at[tokens, pl.ds(s * CORE, CORE)], sibling,
            )

    def cot_wait(s):
        loads["cot", s].wait()
        arrived(("cot", s), cot.at[others, pl.ds(s * CORE, CORE)])

    def b_terms(g):
        if g == 0:
            arrived("low", low_t.at[1 - c])
        for s in range(g * NS, (g + 1) * NS):
            cot_wait(s)
            cols = slice(s * CORE, (s + 1) * CORE)
            term = jnp.dot(low_t[0], cot[:TOK, cols], preferred_element_type=jnp.float32)
            term += jnp.dot(low_t[1], cot[TOK:, cols], preferred_element_type=jnp.float32)
            own[s] = term
            for k in range(NX):
                x_out[k, s] = term[k * PIECE:(k + 1) * PIECE].astype(jnp.bfloat16)
        part = pl.ds(g * NS, NS)
        for k in (1, 3, 2):
            send(
                ("b1", k, g), x_out.at[lax.rem(x + k, NX), part], x_in.at[k - 1, part], at_x(k)
            )

    def b_x_sum():
        mine = pl.ds(pl.multiple_of(x * PIECE, PIECE), PIECE)
        for g in range(NY):
            for k in (1, 3, 2):
                arrived(("b1", k, g), x_in.at[k - 1, pl.ds(g * NS, NS)])
            for zz in range(NS):
                s = g * NS + zz
                total = own[s, mine]
                for k in range(NX - 1):
                    total = total + x_in[k, s].astype(jnp.float32)
                y_own[g, zz] = total
                y_out[g, zz] = total.astype(jnp.bfloat16)
        for k in (1, 3, 2):
            send(("b2", k), y_out.at[lax.rem(y + k, NY)], y_in.at[k - 1], at_y(k))

    def b_y_sum():
        for k in (1, 3, 2):
            arrived(("b2", k), y_in.at[k - 1])
        for zz in range(NS):
            total = y_own[y, zz]
            for k in range(NY - 1):
                total = total + y_in[k, zz].astype(jnp.float32)
            z_own[zz] = total.astype(jnp.bfloat16)
        z_in[z] = z_own[zl]
        for k in range(1, NZ):
            send(("b3", k), z_own.at[lax.rem(zl + k, NS)], z_in.at[z], at_z(k))

    def b_z_sum():
        for k in range(1, NZ):
            arrived(("b3", k), z_in.at[lax.rem(z + NZ - k, NZ)])
        total = z_in[0].astype(jnp.float32)
        for k in range(1, NZ):
            total = total + z_in[k].astype(jnp.float32)
        gath[me8] = total * FACTOR
        for k in range(1, 8):
            send(("b4", k), gath.at[me8], gath.at[me8], at_8(k))

    def b_write():
        for k in range(1, 8):
            arrived(("b4", k), gath.at[lax.rem(me8 + 8 - k, 8)])
        for p in range(8):
            rows, cols = (p // 2) * PIECE, (p % 2) * CORE
            b_done[rows:rows + PIECE, cols:cols + CORE] = gath[p]
        store(b_done, out_b)

    def a_through(*dbs):
        total = None
        for db in dbs:
            for da in (0, -1, 1, 2):
                for j in (0, 1):
                    ys, zs = slot(j, da, db)
                    base = pl.multiple_of((ys * NS + zs) * CORE + j * UNIT, UNIT)
                    term = dot_cols(ubuf[j, ys, zs], cot[:, pl.ds(base, UNIT)])
                    total = term if total is None else total + term
        for core in (0, 1):
            part = total[:, core * TOK:(core + 1) * TOK]
            if 0 in dbs:
                thr[core] = part
            else:
                thr[core] += part

    def a_terms():
        arrived("latent", latent.at[others])
        send("thr", thr.at[1 - c], thr_in, sibling)
        term = jnp.dot(
            thr[0].astype(jnp.bfloat16), latent[:TOK], preferred_element_type=jnp.float32
        )
        term += jnp.dot(
            thr[1].astype(jnp.bfloat16), latent[TOK:], preferred_element_type=jnp.float32
        )
        for p in range(8):
            rows, cols = (p // 2) * PIECE, (p % 2) * (LAT // 2)
            a_own[p] = term[rows:rows + PIECE, cols:cols + LAT // 2]
        for k in range(1, 8):
            send(("a1", k), a_own.at[lax.rem(me8 + k, 8)], a_in.at[k - 1], at_8(k))

    def a_8_sum():
        for k in range(1, 8):
            arrived(("a1", k), a_in.at[k - 1])
        total = a_own[me8]
        for k in range(7):
            total = total + a_in[k]
        ay_in[y] = total
        for k in (1, 3, 2):
            send(("a2", k), ay_in.at[y], ay_in.at[y], at_y(k))

    def a_y_sum():
        for k in (1, 3, 2):
            arrived(("a2", k), ay_in.at[lax.rem(y + NY - k, NY)])
        total = ay_in[0]
        for k in range(1, NY):
            total = total + ay_in[k]
        az_in[z] = total.astype(jnp.bfloat16)
        for k in range(1, NZ):
            send(("a3", k), az_in.at[z], az_in.at[z], at_z(k))

    def a_z_sum():
        for k in range(1, NZ):
            arrived(("a3", k), az_in.at[lax.rem(z + NZ - k, NZ)])
        total = az_in[0].astype(jnp.float32)
        for k in range(1, NZ):
            total = total + az_in[k].astype(jnp.float32)
        a_all[me8] = total * FACTOR
        for k in range(1, 8):
            send(("a4", k), a_all.at[me8], a_all.at[me8], at_8(k))

    def a_write():
        for k in range(1, 8):
            arrived(("a4", k), a_all.at[lax.rem(me8 + 8 - k, 8)])
        for p in range(8):
            rows, cols = (p // 2) * PIECE, (p % 2) * (LAT // 2)
            a_done[rows:rows + PIECE, cols:cols + LAT // 2] = a_all[p]
        store(a_done, out_a)

    def up_wait():
        for j in (0, 1):
            loads["up", j].wait()
        pl.semaphore_wait(barrier, len(partners))

    def take(da, db):
        for j in (0, 1):
            w_take(j, da, db)

    def cross(da, db):
        for j in (0, 1):
            w_cross(j, da, db)

    def second(da):
        for j in (0, 1):
            w_second(j, da)

    def onward(da, db):
        for j in (0, 1):
            w_pass(j, da, db)

    def use(da, db):
        if (da, db) != (0, 0):
            w_ready(da, db)
        w_use(da, db)

    def w_first():
        loads["quant"].wait()
        loads["scales"].wait()
        for j in (0, 1):
            w_start(j)

    up_wait()
    up_start()
    low_start()
    w_first()
    cot_send()
    second(0)
    up_first(-1)
    b_terms(0)
    up_turn(0)
    take(-1, 0)
    up_first(1)
    cross(-1, 0)
    second(-1)
    b_terms(1)
    take(0, -1)
    take(0, 1)
    take(1, 0)
    cross(0, -1)
    up_far()
    b_terms(2)
    up_turn(1)
    second(1)
    up_turn(-1)
    b_terms(3)
    take(-1, 1)
    a_through(0)
    up_turn(2)
    cross(0, 1)
    take(2, 0)
    cross(-1, 1)
    second(2)
    a_through(-1, 1)
    take(1, -1)
    cross(1, -1)
    use(0, 0)
    b_x_sum()
    up_all()
    take(-1, -1)
    onward(0, 1)
    a_through(2)
    take(1, 1)
    onward(0, -1)
    cross(1, 1)
    a_terms()
    onward(-1, 1)
    take(2, 1)
    use(-1, 1)
    cross(1, 0)
    use(0, 1)
    take(2, -1)
    cross(-1, -1)
    cross(2, -1)
    use(0, -1)
    onward(1, -1)
    b_y_sum()
    take(0, 2)
    use(1, -1)
    a_8_sum()
    use(-1, 0)
    use(0, 2)
    cross(2, 1)
    onward(-1, -1)
    onward(1, 1)
    use(-1, -1)
    use(1, 0)
    cross(2, 0)
    use(1, 1)
    a_y_sum()
    b_z_sum()
    onward(2, -1)
    onward(2, 1)
    take(1, 2)
    use(1, 2)
    take(-1, 2)
    use(2, 0)
    use(2, 1)
    use(2, -1)
    use(-1, 2)
    a_z_sum()
    b_write()
    take(2, 2)
    strip = TOK // 2
    for i in (0, 1):
        rows = pl.ds(pl.multiple_of((1 - c) * TOK + i * strip, strip), strip)
        part = pl.ds(i * strip, strip)
        w_use(2, 2, rows)
        acc_out[part] = acc[rows].astype(jnp.bfloat16)
        send(("acc", i), acc_out.at[part], acc_in.at[part], sibling)
    w_use(2, 2, tokens)
    arrived("thr", thr_in)
    through = (thr[c] + thr_in[...]).T.astype(jnp.bfloat16)
    acc[tokens] += jnp.dot(through, down[...], preferred_element_type=jnp.float32)
    a_write()
    for i in (0, 1):
        rows = pl.ds(pl.multiple_of(c * TOK + i * strip, strip), strip)
        part = pl.ds(i * strip, strip)
        arrived(("acc", i), acc_in.at[part])
        lat_done[part] = (acc[rows] + acc_in[part].astype(jnp.float32)).astype(jnp.bfloat16)
        store(lat_done.at[part], out_lat.at[part])
    for copy in sent:
        copy.wait_send()
    for copy in stores:
        copy.wait()


def tidy(lat, grad_a, grad_b, out_lat, out_a, out_b, lat_held, a_held, b_held, in_sem, out_sem):
    moves = ((grad_b, b_held, out_b), (lat, lat_held, out_lat), (grad_a, a_held, out_a))
    reads = [pltpu.make_async_copy(m[0], m[1], in_sem.at[i]) for i, m in enumerate(moves)]
    writes = [pltpu.make_async_copy(m[1], m[2], out_sem.at[i]) for i, m in enumerate(moves)]
    for read in reads:
        read.start()
    for read, write in zip(reads, writes):
        read.wait()
        write.start()
    for write in writes:
        write.wait()


def shards(latent, cotangent, quant, scales, adapter_down, adapter_up):
    hbm = pl.BlockSpec(memory_space=pl.ANY)
    bf16, f32 = jnp.bfloat16, jnp.float32
    results = (
        jax.ShapeDtypeStruct((TOK, LAT), bf16),
        jax.ShapeDtypeStruct((RANK, LAT), f32),
        jax.ShapeDtypeStruct((RANK, SHARD), f32),
    )
    outs = pl.pallas_call(
        kernel,
        name="adapter_backward",
        out_shape=results,
        in_specs=[hbm] * 6,
        out_specs=(hbm, hbm, hbm),
        scratch_shapes=[
            pltpu.VMEM((CHIP, LAT), bf16),
            pltpu.VMEM((RANK, LAT), bf16),
            pltpu.VMEM((LAT, CORE), bf16),
            pltpu.VMEM((CHIP, MINE), bf16),
            pltpu.VMEM((2, NY, NS, LAT, UNIT), bf16),
            pltpu.VMEM((2, NY, NS, RANK, UNIT), bf16),
            pltpu.VMEM((2, RANK, TOK), bf16),
            pltpu.VMEM((CHIP, LAT), f32),
            pltpu.VMEM((TOK, LAT), bf16),
            pltpu.VMEM((TOK, LAT), bf16),
            pltpu.VMEM((2, RANK, TOK), f32),
            pltpu.VMEM((RANK, TOK), f32),
            pltpu.VMEM((SHARDS, RANK, CORE), f32),
            pltpu.VMEM((NX, SHARDS, PIECE, CORE), bf16),
            pltpu.VMEM((NX - 1, SHARDS, PIECE, CORE), bf16),
            pltpu.VMEM((NY, NS, PIECE, CORE), f32),
            pltpu.VMEM((NY, NS, PIECE, CORE), bf16),
            pltpu.VMEM((NY - 1, NS, PIECE, CORE), bf16),
            pltpu.VMEM((NS, PIECE, CORE), bf16),
            pltpu.VMEM((NZ, PIECE, CORE), bf16),
            pltpu.VMEM((8, PIECE, CORE), f32),
            pltpu.VMEM((8, PIECE, LAT // 2), f32),
            pltpu.VMEM((7, PIECE, LAT // 2), f32),
            pltpu.VMEM((NY, PIECE, LAT // 2), f32),
            pltpu.VMEM((NZ, PIECE, LAT // 2), bf16),
            pltpu.VMEM((8, PIECE, LAT // 2), f32),
            pltpu.VMEM((TOK, LAT), bf16),
            pltpu.VMEM((RANK, LAT), f32),
            pltpu.VMEM((RANK, SHARD), f32),
            pltpu.SMEM((LAT // BLOCK, SHARD // BLOCK), f32),
            pltpu.SemaphoreType.DMA((10 + SHARDS,)),
            pltpu.SemaphoreType.DMA((SENDS,)),
            pltpu.SemaphoreType.DMA((RECVS,)),
        ],
        compiler_params=pltpu.CompilerParams(
            collective_id=0, has_side_effects=True, vmem_limit_bytes=56 * 2**20
        ),
        cost_estimate=pl.CostEstimate(
            flops=2 * TOK * COLS * (LAT + 2 * RANK), bytes_accessed=12 * 2**20, transcendentals=0
        ),
    )(scales, latent, cotangent, quant, adapter_down.T, adapter_up)
    lat, grad_a_t, grad_b = pl.pallas_call(
        tidy,
        name="tidy",
        out_shape=results,
        in_specs=[hbm] * 3,
        out_specs=(hbm, hbm, hbm),
        scratch_shapes=[
            pltpu.VMEM((TOK, LAT), bf16),
            pltpu.VMEM((RANK, LAT), f32),
            pltpu.VMEM((RANK, SHARD), f32),
            pltpu.SemaphoreType.DMA((3,)),
            pltpu.SemaphoreType.DMA((3,)),
        ],
    )(*outs)
    return lat, grad_a_t.T, grad_b


def solution(mesh):
    placed = (
        P(("dp", "fsdp"), None),
        P(("dp", "fsdp"), None),
        P(None, "fsdp"),
        P(None, "fsdp"),
        P(),
        P(None, "fsdp"),
    )
    return jax.shard_map(
        shards,
        mesh=mesh,
        in_specs=placed,
        out_specs=(P(("dp", "fsdp"), None), P(), P(None, "fsdp")),
        check_vma=False,
    )
```
